32 devices in a mesh: gx: 16 (over z, y, x), vert: 2 (over core).
Axes of the slice: x: 2, y: 2, z: 4, core: 2. Of those that a mesh axis runs over, the one named last changes fastest.
Arguments:
- start_field: float32 [64, 128, 2048], P('gx', None, 'vert'), may hold values from -6 to 6
- start_collision: float32 [64, 128, 2048], P('gx', None, 'vert'), may hold values from -6 to 6
- inverse: bfloat16 [2048, 2048], P('vert')
- lattice: int32 [2, 2048], P(None, 'vert'), may hold values from -22 to 22
Outputs:
- end_field: float32 [64, 128, 2048], P('gx', None, 'vert')
- end_collision: float32 [64, 128, 2048], P('gx', None, 'vert')
The draws below stay inside these ranges and needn't reach their ends.
All inputs are finite; a program needn't handle non-finite values.
Results may differ from the reference program's by a relative error of at most 0.0095.
Values may be sent and summed in bfloat16 or wider, within the bound.
No kernel may reach another device: no remote copies, remote signals or barrier semaphores. Data moves between devices by JAX's collectives and lax.ppermute only.
A program may use at most 128 MiB of HBM per device.

```python
import jax
import jax.numpy as jnp
from jax import lax

V = 2048
NY = 128
SWEEPS = 2
NX = 64


def draw_inverse(key, part):
    inner = jax.random.fold_in(key, 11)
    key_diag, key_off = jax.random.split(inner)
    spread = 0.25 / V ** 0.5
    diag = jnp.exp(jax.random.uniform(key_diag, (V,), jnp.float32, -1.2, 0.0))
    offdiag = jnp.clip(jax.random.normal(key_off, (V, V), jnp.float32), -4.0, 4.0) * spread
    rows = lax.broadcasted_iota(jnp.int32, (V, V), 0)
    cols = lax.broadcasted_iota(jnp.int32, (V, V), 1)
    result = offdiag + jnp.where(rows == cols, diag[:, None], 0.0)
    return result.astype(jnp.bfloat16)


def touch_ends(entries, rng, least, high):
    extent = entries.shape
    place = [jax.random.randint(jax.random.fold_in(rng, axis), (), 0, extent[axis]) for axis in range(len(extent))]
    entries = entries.at[tuple(place)].set(least)
    longest = extent.index(max(extent))
    place[longest] = (place[longest] + 1) % extent[longest]
    return entries.at[tuple(place)].set(high)


def level_of(rng, dims, shards, low, top_value):
    def one(axis_at, blocks):
        steps = jax.random.uniform(jax.random.fold_in(jax.random.fold_in(rng, 6), axis_at), (blocks,), jnp.float32, low / len(shards), top_value / len(shards))
        return jnp.repeat(jnp.exp(steps), dims[axis_at] // blocks).reshape((-1,) + (1,) * (len(dims) - axis_at - 1))

    level = one(*shards[0])
    for cut in shards[1:]:
        level = level * one(*cut)
    return level


def centred(stream_key, extent, scale, bound, shards=(), kind=jnp.bfloat16):
    array = jax.random.normal(stream_key, extent, jnp.float32) * scale
    if len(shards) > 0:
        array = level_of(stream_key, extent, shards, -0.22, 0.18) * array
    return jnp.clip(array, min=-bound, max=bound).astype(kind)


def setup_inputs(seed: int = 0) -> dict:
    streams_of = jax.random.split(jax.random.key(seed), 5)
    return {
        "start_field": centred(streams_of[0], (NX, NY, V), 1.0, 6.0, ((0, 16), (2, 2)), jnp.float32),
        "start_collision": centred(streams_of[1], (NX, NY, V), 1.0, 6.0, ((0, 16), (2, 2)), jnp.float32),
        "inverse": draw_inverse(jax.random.fold_in(streams_of[4], 71), 0),
        "lattice": touch_ends(jax.random.randint(streams_of[3], (2, V), -22, 23), jax.random.fold_in(streams_of[3], 1), -22, 22).astype(jnp.int32),
    }


step_half = 0.25
step_full = 0.5
lattice_speed = 0.07
near_weight = 5.0 / 24.0
mid_weight = 1.0 / 3.0
far_weight = -1.0 / 24.0


def upwind(minus_two, minus_one, centre, plus_one, plus_two, lattice_row):
    speed = lattice_row.astype(jnp.float32) * lattice_speed
    backward = 1.5 * centre - 2.0 * minus_one + 0.5 * minus_two
    forward = -1.5 * centre + 2.0 * plus_one - 0.5 * plus_two
    return jnp.where(lattice_row > 0, speed * backward, speed * forward)


def transport(field, lattice):
    flux_x = upwind(jnp.roll(field, 2, 0), jnp.roll(field, 1, 0), field, jnp.roll(field, -1, 0), jnp.roll(field, -2, 0), lattice[0])
    flux_y = upwind(jnp.roll(field, 2, 1), jnp.roll(field, 1, 1), field, jnp.roll(field, -1, 1), jnp.roll(field, -2, 1), lattice[1])
    return -(flux_x + flux_y)


def quadrature(drift, relax):
    total = [drift[j] + relax[j] for j in range(3)]
    first = step_full * (near_weight * total[0] + mid_weight * total[1] + far_weight * total[2])
    second = step_full * (far_weight * total[0] + mid_weight * total[1] + near_weight * total[2])
    return first, second


def collide(rounded, inverse):
    flat = rounded.reshape(-1, V).astype(jnp.float32)
    result = jnp.dot(flat, inverse.astype(jnp.float32).T, precision=lax.Precision.HIGHEST)
    return result.reshape(rounded.shape)


def reference(start_field, start_collision, inverse, lattice):
    drift_zero = transport(start_field, lattice)
    drift = [drift_zero, drift_zero, drift_zero]
    relax = [start_collision, start_collision, start_collision]
    field_two = start_field
    for sweep in range(SWEEPS):
        first, second = quadrature(drift, relax)
        rounded_one = (start_field - step_half * relax[1] + first).astype(jnp.bfloat16)
        field_one = collide(rounded_one, inverse)
        relax_one = (field_one - rounded_one.astype(jnp.float32)) / step_half
        drift_one = transport(field_one, lattice)
        rounded_two = (field_one + step_half * (drift_one - drift[1]) - step_half * relax[2] + second).astype(jnp.bfloat16)
        field_two = collide(rounded_two, inverse)
        relax_two = (field_two - rounded_two.astype(jnp.float32)) / step_half
        if sweep + 1 < SWEEPS:
            drift_two = transport(field_two, lattice)
        else:
            drift_two = drift[2]
        drift = [drift_zero, drift_one, drift_two]
        relax = [start_collision, relax_one, relax_two]
    return field_two, relax[2]
```

```python
import jax
import jax.numpy as jnp
from jax import lax
from jax.experimental import pallas as pl
from jax.experimental.pallas import tpu as pltpu
from jax.sharding import PartitionSpec as P

SWEEPS = 2
CHUNKS = 2

step_half = 0.25
step_full = 0.5
lattice_speed = 0.07
near_weight = 5.0 / 24.0
mid_weight = 1.0 / 3.0
far_weight = -1.0 / 24.0

LANES = 128
EDGE = 8
MIB = 1 << 20


def padded_2(cells, axis):
    count = lax.axis_size(axis)
    head = cells[:2].astype(jnp.bfloat16)
    tail = cells[-2:].astype(jnp.bfloat16)
    return jnp.concatenate(
        [
            lax.ppermute(tail, axis, [(i, (i + 1) % count) for i in range(count)]).astype(cells.dtype),
            cells,
            lax.ppermute(head, axis, [((i + 1) % count, i) for i in range(count)]).astype(cells.dtype),
        ],
        axis=0,
    )


def upwind(minus_two, minus_one, centre, plus_one, plus_two, lattice_row):
    speed = lattice_row.astype(jnp.float32) * lattice_speed
    backward = 1.5 * centre - 2.0 * minus_one + 0.5 * minus_two
    forward = -1.5 * centre + 2.0 * plus_one - 0.5 * plus_two
    return jnp.where(lattice_row > 0, speed * backward, speed * forward)


def transport(field, lattice):
    padded = padded_2(field, "gx")
    rows = field.shape[0]
    flux_x = upwind(
        padded[0:rows],
        padded[1 : rows + 1],
        field,
        padded[3 : rows + 3],
        padded[4 : rows + 4],
        lattice[0],
    )
    flux_y = upwind(
        jnp.roll(field, 2, 1),
        jnp.roll(field, 1, 1),
        field,
        jnp.roll(field, -1, 1),
        jnp.roll(field, -2, 1),
        lattice[1],
    )
    return -(flux_x + flux_y)


def quadrature(drift, relax):
    total = [drift[j] + relax[j] for j in range(3)]
    first = step_full * (near_weight * total[0] + mid_weight * total[1] + far_weight * total[2])
    second = step_full * (far_weight * total[0] + mid_weight * total[1] + near_weight * total[2])
    return (first, second)


def swap(cells):
    return lax.ppermute(cells, "vert", [(0, 1), (1, 0)])


def general(start_field, start_collision, mine, other, lattice):
    def collide(rounded):
        beside = swap(rounded)
        return jnp.einsum("xyw,vw->xyv", rounded, mine, preferred_element_type=jnp.float32) + jnp.einsum(
            "xyw,vw->xyv", beside, other, preferred_element_type=jnp.float32
        )

    drift_zero = transport(start_field, lattice)
    drift = [drift_zero, drift_zero, drift_zero]
    relax = [start_collision, start_collision, start_collision]
    field_two = start_field
    for sweep in range(SWEEPS):
        first, second = quadrature(drift, relax)
        rounded_one = (start_field - step_half * relax[1] + first).astype(jnp.bfloat16)
        field_one = collide(rounded_one)
        relax_one = (field_one - rounded_one.astype(jnp.float32)) / step_half
        drift_one = transport(field_one, lattice)
        rounded_two = (
            field_one + step_half * (drift_one - drift[1]) - step_half * relax[2] + second
        ).astype(jnp.bfloat16)
        field_two = collide(rounded_two)
        relax_two = (field_two - rounded_two.astype(jnp.float32)) / step_half
        drift_two = transport(field_two, lattice) if sweep + 1 < SWEEPS else drift[2]
        drift = [drift_zero, drift_one, drift_two]
        relax = [start_collision, relax_one, relax_two]
    return (field_two, relax[2])


def call(body, outs, cost, meta, operands, scratch=()):
    return pl.pallas_call(
        body,
        out_shape=outs,
        in_specs=[pl.BlockSpec(memory_space=pltpu.SMEM)] + [pl.BlockSpec(memory_space=pltpu.VMEM)] * len(operands),
        out_specs=[pl.BlockSpec(memory_space=pltpu.VMEM)] * len(outs),
        scratch_shapes=list(scratch),
        compiler_params=pltpu.CompilerParams(vmem_limit_bytes=16 * MIB),
        cost_estimate=pl.CostEstimate(flops=cost[0], bytes_accessed=cost[1], transcendentals=0),
    )(meta, *operands)


TILE = 256


def product(left, right):
    return lax.dot_general(left, right, (((1,), (0,)), ((), ())), preferred_element_type=jnp.float32)


def product_t(left, right):
    return lax.dot_general(left, right, (((1,), (1,)), ((), ())), preferred_element_type=jnp.float32)


def places(row):
    width = row.shape[1]
    tiles = width // LANES
    value = row.astype(jnp.float32)
    kinds = [value > 0.0, value < 0.0, value == 0.0]
    parts = [
        jnp.where(kind[:, t * LANES : (t + 1) * LANES], 1.0, 0.0) for kind in kinds for t in range(tiles)
    ]
    stacked = jnp.concatenate(parts, axis=0)
    down = lax.broadcasted_iota(jnp.int32, (LANES, LANES), 0)
    along = lax.broadcasted_iota(jnp.int32, (LANES, LANES), 1)
    within = product(stacked, jnp.where(down < along, 1.0, 0.0))
    totals = product(stacked, jnp.ones((LANES, LANES), jnp.float32))
    ranks, sums = [], []
    for kind in range(3):
        base = jnp.zeros((1, LANES), jnp.float32)
        row_ranks = []
        for t in range(tiles):
            at = kind * tiles + t
            row_ranks.append(within[at : at + 1] + base)
            base = base + totals[at : at + 1]
        ranks.append(row_ranks)
        sums.append(base)
    spots = []
    for t in range(tiles):
        at = slice(t * LANES, (t + 1) * LANES)
        spots.append(
            jnp.where(
                kinds[0][:, at],
                ranks[0][t],
                jnp.where(kinds[1][:, at], width - sums[1] + ranks[1][t], sums[0] + ranks[2][t]),
            )
        )
    return jnp.concatenate(spots, axis=1), jnp.maximum(sums[0], sums[1])


def one_hot(spots, low, count):
    width = spots.shape[1]
    down = lax.broadcasted_iota(jnp.int32, (count, width), 0) + low
    return jnp.where(spots.astype(jnp.int32) == down, 1.0, 0.0).astype(jnp.bfloat16)


def put_halo(store, parity, value, low, width, cap, first_row, tail):
    span = value.shape[-1]
    if tail:
        count = min(cap - low, span)
        if count > 0:
            store[parity, :, :, pl.ds(low, count)] = value[first_row : first_row + 2, :, :count]
    else:
        skip = max(width - cap - low, 0)
        if skip < span:
            store[1 - parity, :, :, pl.ds(low + skip - (width - cap), span - skip)] = value[
                first_row : first_row + 2, :, skip:
            ]


def sort_body(meta, lattice, start, *refs):
    hot, main, most = refs[:3]
    sends, store = refs[3:-1], refs[-1]
    rows, cells, width = start.shape
    cap = store.shape[3]
    size = cells // CHUNKS
    parity = meta[0]
    spots, larger = places(lattice[0:1, :])
    most[...] = larger
    narrow = start[...].astype(jnp.bfloat16).reshape(rows * cells, width)
    for low in range(0, width, TILE):
        some = one_hot(spots, low, TILE)
        hot[pl.ds(low, TILE), :] = some
        value = product_t(narrow, some).astype(jnp.bfloat16).reshape(rows, cells, TILE)
        main[:, :, pl.ds(low, TILE)] = value
        put_halo(store, parity, value, low, width, cap, rows - 2, True)
        put_halo(store, parity, value, low, width, cap, 0, False)
    for index in range(CHUNKS):
        for way in range(2):
            sends[2 * index + way][...] = store[way, :, pl.ds(index * size, size), :]


def rest_body(meta, start, collision, hot, main, lattice, weights, *outs):
    del meta
    starts, collisions = outs[:CHUNKS], outs[CHUNKS:]
    rows, cells, width = start.shape
    size = cells // CHUNKS
    both = lattice[...].astype(jnp.float32).astype(jnp.bfloat16)
    sorted_both = product_t(both, hot[...])
    speed = jnp.abs(sorted_both) * lattice_speed
    weights[0:1, :] = -1.5 * (speed[0:1] + speed[1:2])
    weights[1:2, :] = 2.0 * speed[0:1]
    weights[2:3, :] = -0.5 * speed[0:1]
    weights[3:4, :] = 2.0 * speed[1:2]
    weights[4:5, :] = -0.5 * speed[1:2]
    weights[5:7, :] = sorted_both
    weights[7:8, :] = jnp.zeros_like(speed[0:1])
    for index in range(CHUNKS):
        ys = pl.ds(index * size, size)
        exact = start[:, ys, :].reshape(rows * size, width)
        low_part = (exact - exact.astype(jnp.bfloat16).astype(jnp.float32)).astype(jnp.bfloat16)
        other = collision[:, ys, :].reshape(rows * size, width).astype(jnp.bfloat16)
        for low in range(0, width, TILE):
            at = pl.ds(low, TILE)
            some = hot[at, :]
            starts[index][:, :, at] = main[:, ys, at].astype(jnp.float32) + product_t(low_part, some).reshape(
                rows, size, TILE
            )
            collisions[index][:, :, at] = (
                product_t(other, some).astype(jnp.bfloat16).reshape(rows, size, TILE)
            )


def inverse_body(meta, lattice, most_in, inverse, hot, own_last, other_last, own, other, most, hot_other):
    width = hot.shape[0]
    spots, larger = places(lattice[0:1, :])
    most[...] = jnp.maximum(larger, most_in[...])
    for low in range(0, width, TILE):
        hot_other[pl.ds(low, TILE), :] = one_hot(spots, low, TILE)
    for source, last, final, place in (
        (hot, own_last, own, meta[1]),
        (hot_other, other_last, other, 1 - meta[1]),
    ):
        columns = inverse[:, pl.ds(pl.multiple_of(place * width, width), width)]
        for low in range(0, width, TILE):
            at = pl.ds(low, TILE)
            value = product_t(source[at, :], columns).astype(jnp.bfloat16)
            last[at, :] = value
            for far in range(0, width, TILE):
                to = pl.ds(far, TILE)
                final[at, to] = product_t(value, hot[to, :]).astype(jnp.bfloat16)


def drift_at(row, lanes, refs, halo, parity):
    field, before, after, weights = refs
    rows, size, width = field.shape
    cap = halo.shape[3]
    low, high = lanes, lanes + LANES
    at = pl.ds(low, LANES)
    centre = field[row, :, at]

    def behind(step):
        source = row - step
        if source >= 0:
            return field[source, :, at]
        return halo[1 - parity, 2 + source, :, at].astype(jnp.float32)

    def ahead(step):
        source = row + step
        if source < rows:
            return field[source, :, at]
        return halo[parity, source - rows, :, pl.ds(low - (width - cap), LANES)].astype(jnp.float32)

    def one(step):
        if high <= width - cap:
            return behind(step)
        if low >= cap:
            return ahead(step)
        return jnp.where(weights[5:6, at] > 0.0, behind(step), ahead(step))

    long = jnp.concatenate(
        [before[row, before.shape[1] - EDGE :, at], centre, after[row, 0:EDGE, at]], axis=0
    )
    up = weights[6:7, at] > 0.0

    def beside(step):
        return jnp.where(up, long[EDGE - step : EDGE - step + size], long[EDGE + step : EDGE + step + size])

    total = weights[0:1, at] * centre
    total = total + weights[1:2, at] * one(1) + weights[2:3, at] * one(2)
    total = total + weights[3:4, at] * beside(1) + weights[4:5, at] * beside(2)
    return centre, total


def drifts(refs):
    meta, field, before, after, weights, from_a, from_b = refs[:7]
    halo = refs[-1]
    parity = meta[0]
    halo[0] = from_a[...]
    halo[1] = from_b[...]
    rows, _, width = field.shape

    def every():
        for lanes in range(0, width, LANES):
            for row in range(rows):
                at = (row, slice(None), pl.ds(lanes, LANES))
                yield (at, *drift_at(row, lanes, (field, before, after, weights), halo, parity))

    return refs[7:-1], every()


def stage_one(*refs):
    (rounded, drift), every = drifts(refs)
    for at, centre, total in every:
        drift[at] = total
        rounded[at] = (centre + step_half * total).astype(jnp.bfloat16)


def stage_two(*refs):
    (start, collision, drift, rounded_one, rounded, part_one, part_two), every = drifts(refs)
    for at, centre, total in every:
        rounded[at] = (centre + step_half * total).astype(jnp.bfloat16)
        change = centre - rounded_one[at].astype(jnp.float32)
        zero = drift[at] + collision[at].astype(jnp.float32)
        part_one[at] = start[at] + (5.0 / 48.0) * zero + (1.0 / 6.0) * total - (1.0 / 3.0) * change
        part_two[at] = (2.0 / 3.0) * change - (1.0 / 48.0) * zero - (1.0 / 12.0) * total


def stage_three(*refs):
    (rounded_two, part_one, part_two, rounded, rest), every = drifts(refs)
    for at, centre, total in every:
        change = centre - rounded_two[at].astype(jnp.float32)
        rounded[at] = (part_one[at] - (1.0 / 48.0) * total - (1.0 / 12.0) * change).astype(jnp.bfloat16)
        rest[at] = part_two[at] + (5.0 / 48.0) * total - (7.0 / 12.0) * change


def stage_four(*refs):
    (rest, rounded), every = drifts(refs)
    for at, centre, total in every:
        rounded[at] = (centre + step_half * total + rest[at]).astype(jnp.bfloat16)


def collide_body(meta, mine, beside, own, other, field, to_a, to_b, store):
    rows, size, width = field.shape
    cap = store.shape[3]
    parity = meta[0]
    first = mine[...].reshape(rows * size, width)
    second = beside[...].reshape(rows * size, width)
    for low in range(0, width, TILE):
        at = pl.ds(low, TILE)
        result = (product(first, own[:, at]) + product(second, other[:, at])).reshape(rows, size, TILE)
        field[:, :, at] = result
        narrow = result.astype(jnp.bfloat16)
        put_halo(store, parity, narrow, low, width, cap, rows - 2, True)
        put_halo(store, parity, narrow, low, width, cap, 0, False)
    to_a[...] = store[0]
    to_b[...] = store[1]


def unsort_body(meta, rounded, hot, plain):
    del meta
    rows, size, width = rounded.shape
    first = rounded[...].reshape(rows * size, width)
    for low in range(0, width, TILE):
        at = pl.ds(low, TILE)
        plain[:, :, at] = product(first, hot[:, at]).astype(jnp.bfloat16).reshape(rows, size, TILE)


def last_body(*refs):
    mine, beside, plain = refs[:CHUNKS], refs[CHUNKS : 2 * CHUNKS], refs[2 * CHUNKS : 3 * CHUNKS]
    own, other, field, collision = refs[3 * CHUNKS :]
    at = pl.ds(pl.multiple_of(pl.program_id(0) * TILE, TILE), TILE)
    for index in range(CHUNKS):
        rows, size, width = mine[index].shape
        first = mine[index][...].reshape(rows * size, width)
        second = beside[index][...].reshape(rows * size, width)
        result = (product(first, own[:, at]) + product(second, other[:, at])).reshape(rows, size, TILE)
        ys = pl.ds(index * size, size)
        field[:, ys, :] = result
        collision[:, ys, :] = (result - plain[index][:, :, at].astype(jnp.float32)) * (1.0 / step_half)


def sorted_path(cap, start_field, start_collision, inverse, lattice):
    rows, cells, width = start_field.shape
    size = cells // CHUNKS
    count = lax.axis_size("gx")
    here = lax.axis_index("gx")
    pairs_a = [(i, i ^ 1) for i in range(count)]
    pairs_b = [(i, (i + 1 if i % 2 else i - 1) % count) for i in range(count)]
    meta = jnp.stack([here % 2, lax.axis_index("vert")]).astype(jnp.int32)
    narrow = jnp.bfloat16

    def shape(dims, dtype=jnp.float32):
        return jax.ShapeDtypeStruct(dims, dtype)

    halo_shape = shape((2, size, cap), narrow)
    square = shape((width, width), narrow)
    wide_shape = shape((rows, size, width))
    thin_shape = shape((rows, size, width), narrow)
    most_shape = shape((1, LANES))
    elements = rows * size * width

    def exchange(to_a, to_b):
        return lax.ppermute(to_a, "gx", pairs_a), lax.ppermute(to_b, "gx", pairs_b)

    beside_lattice = swap(lattice)
    hot, main, most_mine, *sends = call(
        sort_body,
        [square, shape((rows, cells, width), narrow), most_shape] + [halo_shape] * (2 * CHUNKS),
        (4 * elements * width, 16 * elements),
        meta,
        (lattice, start_field),
        [pltpu.VMEM((2, 2, cells, cap), narrow)],
    )
    halos = [exchange(*sends[2 * index : 2 * index + 2]) for index in range(CHUNKS)]
    weights, *sorted_parts = call(
        rest_body,
        [shape((8, width))] + [wide_shape] * CHUNKS + [thin_shape] * CHUNKS,
        (8 * elements * width, 40 * elements),
        meta,
        (start_field, start_collision, hot, main, lattice),
    )
    starts, collisions = sorted_parts[:CHUNKS], sorted_parts[CHUNKS:]
    own_last, other_last, own, other, most = call(
        inverse_body,
        [square] * 4 + [most_shape],
        (8 * width**3, 20 * width**2),
        meta,
        (beside_lattice, most_mine, inverse, hot),
        [pltpu.VMEM((width, width), narrow)],
    )

    def stage(body, outs, fields, index, *extra):
        around = (fields[index - 1], fields[(index + 1) % CHUNKS])
        return call(
            body,
            outs,
            (30 * elements, 16 * elements),
            meta,
            (fields[index], *around, weights, *halos[index], *extra),
            [pltpu.VMEM((2, 2, size, cap), narrow)],
        )

    def advance(rounded):
        results = [
            call(
                collide_body,
                [wide_shape, halo_shape, halo_shape],
                (4 * elements * width, 8 * elements + 4 * width * width),
                meta,
                (r, swap(r), own, other),
                [pltpu.VMEM((2, 2, size, cap), narrow)],
            )
            for r in rounded
        ]
        return [r[0] for r in results], [exchange(r[1], r[2]) for r in results]

    every = range(CHUNKS)
    fields = starts
    kept = [stage(stage_one, [thin_shape, wide_shape], fields, i) for i in every]
    fields, halos = advance([k[0] for k in kept])
    kept = [
        stage(
            stage_two,
            [thin_shape, wide_shape, wide_shape],
            fields,
            i,
            starts[i],
            collisions[i],
            kept[i][1],
            kept[i][0],
        )
        for i in every
    ]
    fields, halos = advance([k[0] for k in kept])
    kept = [stage(stage_three, [thin_shape, wide_shape], fields, i, *kept[i]) for i in every]
    fields, halos = advance([k[0] for k in kept])
    rounded = [stage(stage_four, [thin_shape], fields, i, kept[i][1])[0] for i in every]
    beside = [swap(r) for r in rounded]
    plain = [
        call(unsort_body, [thin_shape], (2 * elements * width, 4 * elements), meta, (r, hot))[0] for r in rounded
    ]
    operands = (*rounded, *beside, *plain, own_last, other_last)
    ends = pl.pallas_call(
        last_body,
        grid=(width // TILE,),
        out_shape=[shape((rows, cells, width))] * 2,
        in_specs=[pl.BlockSpec(memory_space=pltpu.VMEM)] * len(operands),
        out_specs=[pl.BlockSpec((rows, cells, TILE), lambda i: (0, 0, i))] * 2,
        compiler_params=pltpu.CompilerParams(vmem_limit_bytes=16 * MIB),
        cost_estimate=pl.CostEstimate(
            flops=4 * CHUNKS * elements * width, bytes_accessed=12 * CHUNKS * elements, transcendentals=0
        ),
    )(*operands)
    return (*ends, most[0, 0] > cap)


def per_device(start_field, start_collision, inverse, lattice):
    width = start_field.shape[2]
    cap = width // 8 * 5
    field, collision, crowded = sorted_path(cap, start_field, start_collision, inverse, lattice)

    def again(state):
        here = lax.axis_index("vert")
        mine = lax.dynamic_slice_in_dim(inverse, here * width, width, axis=1)
        other = lax.dynamic_slice_in_dim(inverse, (1 - here) * width, width, axis=1)
        return (*general(start_field, start_collision, mine, other, lattice), jnp.zeros((), jnp.bool_))

    field, collision, _ = lax.while_loop(lambda state: state[2], again, (field, collision, crowded))
    return field, collision


def solution(mesh):
    return jax.shard_map(
        per_device,
        mesh=mesh,
        in_specs=(P("gx", None, "vert"), P("gx", None, "vert"), P("vert", None), P(None, "vert")),
        out_specs=(P("gx", None, "vert"), P("gx", None, "vert")),
        check_vma=False,
    )
```

```python
import jax
import jax.numpy as jnp
from jax import lax
from jax.experimental import pallas as pl
from jax.experimental.pallas import tpu as pltpu
from jax.sharding import PartitionSpec as P

SWEEPS = 2
CHUNKS = 2

step_half = 0.25
step_full = 0.5
lattice_speed = 0.07
near_weight = 5.0 / 24.0
mid_weight = 1.0 / 3.0
far_weight = -1.0 / 24.0

LANES = 128
EDGE = 8
MIB = 1 << 20


def padded_2(cells, axis):
    count = lax.axis_size(axis)
    head = cells[:2].astype(jnp.bfloat16)
    tail = cells[-2:].astype(jnp.bfloat16)
    return jnp.concatenate(
        [
            lax.ppermute(tail, axis, [(i, (i + 1) % count) for i in range(count)]).astype(cells.dtype),
            cells,
            lax.ppermute(head, axis, [((i + 1) % count, i) for i in range(count)]).astype(cells.dtype),
        ],
        axis=0,
    )


def upwind(minus_two, minus_one, centre, plus_one, plus_two, lattice_row):
    speed = lattice_row.astype(jnp.float32) * lattice_speed
    backward = 1.5 * centre - 2.0 * minus_one + 0.5 * minus_two
    forward = -1.5 * centre + 2.0 * plus_one - 0.5 * plus_two
    return jnp.where(lattice_row > 0, speed * backward, speed * forward)


def transport(field, lattice):
    padded = padded_2(field, "gx")
    rows = field.shape[0]
    flux_x = upwind(
        padded[0:rows],
        padded[1 : rows + 1],
        field,
        padded[3 : rows + 3],
        padded[4 : rows + 4],
        lattice[0],
    )
    flux_y = upwind(
        jnp.roll(field, 2, 1),
        jnp.roll(field, 1, 1),
        field,
        jnp.roll(field, -1, 1),
        jnp.roll(field, -2, 1),
        lattice[1],
    )
    return -(flux_x + flux_y)


def quadrature(drift, relax):
    total = [drift[j] + relax[j] for j in range(3)]
    first = step_full * (near_weight * total[0] + mid_weight * total[1] + far_weight * total[2])
    second = step_full * (far_weight * total[0] + mid_weight * total[1] + near_weight * total[2])
    return (first, second)


def swap(cells):
    return lax.ppermute(cells, "vert", [(0, 1), (1, 0)])


def general(start_field, start_collision, mine, other, lattice):
    def collide(rounded):
        beside = swap(rounded)
        return jnp.einsum("xyw,vw->xyv", rounded, mine, preferred_element_type=jnp.float32) + jnp.einsum(
            "xyw,vw->xyv", beside, other, preferred_element_type=jnp.float32
        )

    drift_zero = transport(start_field, lattice)
    drift = [drift_zero, drift_zero, drift_zero]
    relax = [start_collision, start_collision, start_collision]
    field_two = start_field
    for sweep in range(SWEEPS):
        first, second = quadrature(drift, relax)
        rounded_one = (start_field - step_half * relax[1] + first).astype(jnp.bfloat16)
        field_one = collide(rounded_one)
        relax_one = (field_one - rounded_one.astype(jnp.float32)) / step_half
        drift_one = transport(field_one, lattice)
        rounded_two = (
            field_one + step_half * (drift_one - drift[1]) - step_half * relax[2] + second
        ).astype(jnp.bfloat16)
        field_two = collide(rounded_two)
        relax_two = (field_two - rounded_two.astype(jnp.float32)) / step_half
        drift_two = transport(field_two, lattice) if sweep + 1 < SWEEPS else drift[2]
        drift = [drift_zero, drift_one, drift_two]
        relax = [start_collision, relax_one, relax_two]
    return (field_two, relax[2])


def call(body, outs, cost, meta, operands, scratch=()):
    return pl.pallas_call(
        body,
        out_shape=outs,
        in_specs=[pl.BlockSpec(memory_space=pltpu.SMEM)] + [pl.BlockSpec(memory_space=pltpu.VMEM)] * len(operands),
        out_specs=[pl.BlockSpec(memory_space=pltpu.VMEM)] * len(outs),
        scratch_shapes=list(scratch),
        compiler_params=pltpu.CompilerParams(vmem_limit_bytes=16 * MIB),
        cost_estimate=pl.CostEstimate(flops=cost[0], bytes_accessed=cost[1], transcendentals=0),
    )(meta, *operands)


TILE = 256


def product(left, right):
    return lax.dot_general(left, right, (((1,), (0,)), ((), ())), preferred_element_type=jnp.float32)


def product_t(left, right):
    return lax.dot_general(left, right, (((1,), (1,)), ((), ())), preferred_element_type=jnp.float32)


def places(row):
    width = row.shape[1]
    tiles = width // LANES
    value = row.astype(jnp.float32)
    kinds = [value > 0.0, value < 0.0, value == 0.0]
    parts = [
        jnp.where(kind[:, t * LANES : (t + 1) * LANES], 1.0, 0.0) for kind in kinds for t in range(tiles)
    ]
    stacked = jnp.concatenate(parts, axis=0)
    down = lax.broadcasted_iota(jnp.int32, (LANES, LANES), 0)
    along = lax.broadcasted_iota(jnp.int32, (LANES, LANES), 1)
    within = product(stacked, jnp.where(down < along, 1.0, 0.0))
    totals = product(stacked, jnp.ones((LANES, LANES), jnp.float32))
    ranks, sums = [], []
    for kind in range(3):
        base = jnp.zeros((1, LANES), jnp.float32)
        row_ranks = []
        for t in range(tiles):
            at = kind * tiles + t
            row_ranks.append(within[at : at + 1] + base)
            base = base + totals[at : at + 1]
        ranks.append(row_ranks)
        sums.append(base)
    spots = []
    for t in range(tiles):
        at = slice(t * LANES, (t + 1) * LANES)
        spots.append(
            jnp.where(
                kinds[0][:, at],
                ranks[0][t],
                jnp.where(kinds[1][:, at], width - sums[1] + ranks[1][t], sums[0] + ranks[2][t]),
            )
        )
    return jnp.concatenate(spots, axis=1), jnp.maximum(sums[0], sums[1])


def one_hot(spots, low, count):
    width = spots.shape[1]
    down = lax.broadcasted_iota(jnp.int32, (count, width), 0) + low
    return jnp.where(spots.astype(jnp.int32) == down, 1.0, 0.0).astype(jnp.bfloat16)


def each_tile(width):
    def run(body):
        for low in range(0, width, TILE):
            body(low)

    return run


def put_halo(tail, head, value, low, ys=slice(None)):
    rows, _, span = value.shape
    cap = tail.shape[2]
    count = min(cap - low, span)
    if count > 0:
        tail[:, :, pl.ds(low, count)] = value[rows - 2 :, ys, :count]
    start = low - head_lane(cap)
    skip = max(-start, 0)
    if skip < span:
        head[:, :, pl.ds(start + skip, span - skip)] = value[:2, ys, skip:]


def head_lane(cap):
    return cap // 5 * 3


def sort_body(meta, lattice, start, *refs):
    hot, main, most, spots_at = *refs[:3], refs[-1]
    sends = refs[3:-1]
    rows, cells, width = start.shape
    size = cells // CHUNKS
    spots, larger = places(lattice[0:1, :])
    most[...] = jnp.broadcast_to(larger, most.shape)
    spots_at[...] = jnp.broadcast_to(spots, spots_at.shape)
    narrow = start[...].astype(jnp.bfloat16).reshape(rows * cells, width)

    @each_tile(width)
    def _(low):
        some = one_hot(spots_at[0:1, :], low, TILE)
        at = pl.ds(low, TILE)
        hot[at, :] = some
        value = product_t(narrow, some).astype(jnp.bfloat16).reshape(rows, cells, TILE)
        main[:, :, at] = value
        for index in range(CHUNKS):
            put_halo(*sends[2 * index : 2 * index + 2], value, low, slice(index * size, (index + 1) * size))


def weights_body(meta, hot, lattice, weights):
    del meta
    both = lattice[...].astype(jnp.float32).astype(jnp.bfloat16)
    sorted_both = product_t(both, hot[...])
    speed = jnp.abs(sorted_both) * lattice_speed
    weights[0:1, :] = -1.5 * (speed[0:1] + speed[1:2])
    weights[1:2, :] = 2.0 * speed[0:1]
    weights[2:3, :] = -0.5 * speed[0:1]
    weights[3:4, :] = 2.0 * speed[1:2]
    weights[4:5, :] = -0.5 * speed[1:2]
    weights[5:7, :] = sorted_both
    weights[7:8, :] = jnp.zeros_like(speed[0:1])


def rest_body(meta, collision, hot, token, out):
    del meta, token
    rows, cells, width = collision.shape
    narrow = collision[...].astype(jnp.bfloat16).reshape(rows * cells, width)

    @each_tile(width)
    def _(low):
        at = pl.ds(low, TILE)
        out[:, :, at] = product_t(narrow, hot[at, :]).astype(jnp.bfloat16).reshape(rows, cells, TILE)


def inverse_body(meta, lattice, most, inverse, hot, own_last, other_last, own, other, token, hot_other, spots_at):
    width = hot.shape[0]
    spots, larger = places(lattice[0:1, :])
    token[...] = jnp.maximum(most[...], larger)
    spots_at[...] = jnp.broadcast_to(spots, spots_at.shape)

    @each_tile(width)
    def _(low):
        hot_other[pl.ds(low, TILE), :] = one_hot(spots_at[0:1, :], low, TILE)

    for source, last, final, place in (
        (hot, own_last, own, meta[0]),
        (hot_other, other_last, other, 1 - meta[0]),
    ):
        columns = pl.ds(pl.multiple_of(place * width, width), width)

        for low in range(0, width, TILE):
            at = pl.ds(low, TILE)
            value = product_t(source[at, :], inverse[:, columns]).astype(jnp.bfloat16)
            last[at, :] = value
            for far in range(0, width, TILE):
                to = pl.ds(far, TILE)
                final[at, to] = product_t(value, hot[to, :]).astype(jnp.bfloat16)


def drift_at(row, at, region, refs, left, right):
    field, before, after, weights = refs
    rows, size, _ = field.shape
    centre = field[row, :, at]

    def behind(step):
        source = row - step
        if source >= 0:
            return field[source, :, at].astype(jnp.float32)
        return left[2 + source]

    def ahead(step):
        source = row + step
        if source < rows:
            return field[source, :, at].astype(jnp.float32)
        return right[source - rows]

    def one(step):
        if region == 0:
            return behind(step)
        if region == 2:
            return ahead(step)
        return jnp.where(weights[5:6, at] > 0.0, behind(step), ahead(step))

    long = jnp.concatenate(
        [
            before[row, before.shape[1] - EDGE :, at].astype(jnp.float32),
            centre.astype(jnp.float32),
            after[row, 0:EDGE, at].astype(jnp.float32),
        ],
        axis=0,
    )
    centre = centre.astype(jnp.float32)
    up = weights[6:7, at] > 0.0

    def beside(step):
        return jnp.where(up, long[EDGE - step : EDGE - step + size], long[EDGE + step : EDGE + step + size])

    total = weights[0:1, at] * centre
    total = total + weights[1:2, at] * one(1) + weights[2:3, at] * one(2)
    total = total + weights[3:4, at] * beside(1) + weights[4:5, at] * beside(2)
    return centre, total


def drifts(fields, refs, body):
    weights, from_last, from_next = refs[:3]
    rows, _, width = fields[0].shape
    cap = from_last.shape[2]
    low = width - cap
    ends = (0, (width - cap) // LANES, cap // LANES, width // LANES)
    for region in range(3):

        for index in range(ends[region], ends[region + 1]):
            at = pl.ds(index * LANES, LANES)
            left, right = None, None
            if region < 2:
                left = [from_last[i, :, at].astype(jnp.float32) for i in range(2)]
            if region > 0:
                beyond = pl.ds(index * LANES - low, LANES)
                right = [from_next[i, :, beyond].astype(jnp.float32) for i in range(2)]
            for row in range(rows):
                body((row, slice(None), at), *drift_at(row, at, region, (*fields, weights), left, right))


def part(ref, index):
    size = ref.shape[1] // CHUNKS
    return ref.at[:, pl.ds(index % CHUNKS * size, size), :]


def stage_one(index):
    def kernel(meta, start, *refs):
        del meta
        _, rounded, drift = refs[3:]

        def body(at, centre, total):
            drift[at] = total
            rounded[at] = (centre + step_half * total).astype(jnp.bfloat16)

        drifts((part(start, index), part(start, index - 1), part(start, index + 1)), refs, body)

    return kernel


def stage_two(index):
    def kernel(meta, field, before, after, *refs):
        del meta
        start, collision, drift, rounded_one, rounded, part_one, part_two = refs[3:]
        start, collision = part(start, index), part(collision, index)

        def body(at, centre, total):
            rounded[at] = (centre + step_half * total).astype(jnp.bfloat16)
            change = centre - rounded_one[at].astype(jnp.float32)
            zero = drift[at] + collision[at].astype(jnp.float32)
            base = start[at].astype(jnp.float32)
            part_one[at] = base + (5.0 / 48.0) * zero + (1.0 / 6.0) * total - (1.0 / 3.0) * change
            part_two[at] = (2.0 / 3.0) * change - (1.0 / 48.0) * zero - (1.0 / 12.0) * total

        drifts((field, before, after), refs, body)

    return kernel


def stage_three(index):
    del index

    def kernel(meta, field, before, after, *refs):
        del meta
        rounded_two, part_one, part_two, rounded, rest = refs[3:]

        def body(at, centre, total):
            change = centre - rounded_two[at].astype(jnp.float32)
            rounded[at] = (part_one[at] - (1.0 / 48.0) * total - (1.0 / 12.0) * change).astype(jnp.bfloat16)
            rest[at] = part_two[at] + (5.0 / 48.0) * total - (7.0 / 12.0) * change

        drifts((field, before, after), refs, body)

    return kernel


def stage_four(index):
    del index

    def kernel(meta, field, before, after, *refs):
        del meta
        rest, rounded = refs[3:]

        def body(at, centre, total):
            rounded[at] = (centre + step_half * total + rest[at]).astype(jnp.bfloat16)

        drifts((field, before, after), refs, body)

    return kernel


def collide_body(meta, mine, beside, own, other, field, to_next, to_last, token):
    del meta
    rows, size, width = field.shape

    @each_tile(width)
    def _(low):
        at = pl.ds(low, TILE)
        first = mine[...].reshape(rows * size, width)
        second = beside[...].reshape(rows * size, width)
        result = (product(first, own[:, at]) + product(second, other[:, at])).reshape(rows, size, TILE)
        field[:, :, at] = result
        put_halo(to_next, to_last, result.astype(jnp.bfloat16), low)

    token[...] = jnp.zeros_like(token)


def unsort_body(meta, rounded, hot, plain):
    del meta
    rows, size, width = rounded.shape
    first = rounded[...].reshape(rows * size, width)

    @each_tile(width)
    def _(low):
        at = pl.ds(low, TILE)
        plain[:, :, at] = product(first, hot[:, at]).astype(jnp.bfloat16).reshape(rows, size, TILE)


def last_body(*refs):
    mine, beside, plain = refs[:CHUNKS], refs[CHUNKS : 2 * CHUNKS], refs[2 * CHUNKS : 3 * CHUNKS]
    own, other, field, collision = refs[3 * CHUNKS :]
    at = pl.ds(pl.multiple_of(pl.program_id(0) * TILE, TILE), TILE)
    for index in range(CHUNKS):
        rows, size, width = mine[index].shape
        first = mine[index][...].reshape(rows * size, width)
        second = beside[index][...].reshape(rows * size, width)
        result = (product(first, own[:, at]) + product(second, other[:, at])).reshape(rows, size, TILE)
        ys = pl.ds(index * size, size)
        field[:, ys, :] = result
        collision[:, ys, :] = (result - plain[index][:, :, at].astype(jnp.float32)) * (1.0 / step_half)


def sorted_path(cap, start_field, start_collision, inverse, lattice):
    rows, cells, width = start_field.shape
    size = cells // CHUNKS
    count = lax.axis_size("gx")
    forth = [(i, (i + 1) % count) for i in range(count)]
    back = [((i + 1) % count, i) for i in range(count)]
    meta = lax.axis_index("vert").astype(jnp.int32).reshape(1)
    narrow = jnp.bfloat16

    def shape(dims, dtype=jnp.float32):
        return jax.ShapeDtypeStruct(dims, dtype)

    halo_shape = shape((2, size, cap), narrow)
    square = shape((width, width), narrow)
    wide_shape = shape((rows, size, width))
    thin_shape = shape((rows, size, width), narrow)
    token_shape = shape((8, LANES))
    elements = rows * size * width

    def exchange(to_next, to_last):
        return lax.ppermute(to_next, "gx", forth), lax.ppermute(to_last, "gx", back)

    beside_lattice = swap(lattice)
    hot, main, most, *sends = call(
        sort_body,
        [square, shape((rows, cells, width), narrow), token_shape] + [halo_shape] * (2 * CHUNKS),
        (4 * elements * width, 16 * elements),
        meta,
        (lattice, start_field),
        [pltpu.VMEM((8, width), jnp.float32)],
    )
    halos = [exchange(*sends[2 * index : 2 * index + 2]) for index in range(CHUNKS)]
    (weights,) = call(weights_body, [shape((8, width))], (1, 1), meta, (hot, lattice))
    own_last, other_last, own, other, largest = call(
        inverse_body,
        [square] * 4 + [token_shape],
        (8 * width**3, 20 * width**2),
        meta,
        (beside_lattice, most, inverse, hot),
        [pltpu.VMEM((width, width), narrow), pltpu.VMEM((8, width), jnp.float32)],
    )

    def stage(body, outs, fields, index, *extra):
        return call(
            body(index),
            outs,
            (30 * elements, 16 * elements),
            meta,
            (*fields, weights, *halos[index], *extra),
        )

    def advance(rounded):
        results = [
            call(
                collide_body,
                [wide_shape, halo_shape, halo_shape, token_shape],
                (4 * elements * width, 8 * elements + 4 * width * width),
                meta,
                (r, swap(r), own, other),
            )
            for r in rounded
        ]
        return [r[0] for r in results], [exchange(r[1], r[2]) for r in results], results[-1][3]

    def around(index):
        return fields[index], fields[index - 1], fields[(index + 1) % CHUNKS]

    every = range(CHUNKS)
    kept = [stage(stage_one, [thin_shape, wide_shape], (main,), i, largest) for i in every]
    fields, halos, token = advance([k[0] for k in kept])
    crowded = largest[0, 0] > cap
    late = jnp.concatenate([meta, crowded.astype(jnp.int32).reshape(1)])
    (collision,) = call(
        rest_body,
        [shape((rows, cells, width), narrow)],
        (2 * CHUNKS * elements * width, 6 * CHUNKS * elements),
        late,
        (start_collision, hot, token),
    )
    kept = [
        stage(
            stage_two, [thin_shape, wide_shape, wide_shape], around(i), i, main, collision, kept[i][1], kept[i][0]
        )
        for i in every
    ]
    fields, halos, token = advance([k[0] for k in kept])
    kept = [stage(stage_three, [thin_shape, wide_shape], around(i), i, *kept[i]) for i in every]
    fields, halos, token = advance([k[0] for k in kept])
    rounded = [stage(stage_four, [thin_shape], around(i), i, kept[i][1])[0] for i in every]
    beside = [swap(r) for r in rounded]
    plain = [
        call(unsort_body, [thin_shape], (2 * elements * width, 4 * elements), meta, (r, hot))[0] for r in rounded
    ]
    operands = (*rounded, *beside, *plain, own_last, other_last)
    ends = pl.pallas_call(
        last_body,
        grid=(width // TILE,),
        out_shape=[shape((rows, cells, width))] * 2,
        in_specs=[pl.BlockSpec(memory_space=pltpu.VMEM)] * len(operands),
        out_specs=[pl.BlockSpec((rows, cells, TILE), lambda i: (0, 0, i))] * 2,
        compiler_params=pltpu.CompilerParams(vmem_limit_bytes=16 * MIB),
        cost_estimate=pl.CostEstimate(
            flops=4 * CHUNKS * elements * width, bytes_accessed=12 * CHUNKS * elements, transcendentals=0
        ),
    )(*operands)
    return (*ends, crowded)


def per_device(start_field, start_collision, inverse, lattice):
    width = start_field.shape[2]
    cap = width // 8 * 5
    field, collision, crowded = sorted_path(cap, start_field, start_collision, inverse, lattice)

    def again(state):
        here = lax.axis_index("vert")
        mine = lax.dynamic_slice_in_dim(inverse, here * width, width, axis=1)
        other = lax.dynamic_slice_in_dim(inverse, (1 - here) * width, width, axis=1)
        return (*general(start_field, start_collision, mine, other, lattice), jnp.zeros((), jnp.bool_))

    field, collision, _ = lax.while_loop(lambda state: state[2], again, (field, collision, crowded))
    return field, collision


def solution(mesh):
    return jax.shard_map(
        per_device,
        mesh=mesh,
        in_specs=(P("gx", None, "vert"), P("gx", None, "vert"), P("vert", None), P(None, "vert")),
        out_specs=(P("gx", None, "vert"), P("gx", None, "vert")),
        check_vma=False,
    )
```

```python
import jax
import jax.numpy as jnp
from jax import lax
from jax.experimental import pallas as pl
from jax.experimental.pallas import tpu as pltpu
from jax.sharding import PartitionSpec as P

CHUNKS = 2

step_half = 0.25
lattice_speed = 0.07

LANES = 128
EDGE = 8
MIB = 1 << 20


def padded_2(cells, axis):
    count = lax.axis_size(axis)
    head = cells[:2].astype(jnp.bfloat16)
    tail = cells[-2:].astype(jnp.bfloat16)
    return jnp.concatenate(
        [
            lax.ppermute(tail, axis, [(i, (i + 1) % count) for i in range(count)]).astype(cells.dtype),
            cells,
            lax.ppermute(head, axis, [((i + 1) % count, i) for i in range(count)]).astype(cells.dtype),
        ],
        axis=0,
    )


def upwind(minus_two, minus_one, centre, plus_one, plus_two, lattice_row):
    speed = lattice_row.astype(jnp.float32) * lattice_speed
    backward = 1.5 * centre - 2.0 * minus_one + 0.5 * minus_two
    forward = -1.5 * centre + 2.0 * plus_one - 0.5 * plus_two
    return jnp.where(lattice_row > 0, speed * backward, speed * forward)


def transport(field, lattice):
    padded = padded_2(field, "gx")
    rows = field.shape[0]
    flux_x = upwind(
        padded[0:rows],
        padded[1 : rows + 1],
        field,
        padded[3 : rows + 3],
        padded[4 : rows + 4],
        lattice[0],
    )
    flux_y = upwind(
        jnp.roll(field, 2, 1),
        jnp.roll(field, 1, 1),
        field,
        jnp.roll(field, -1, 1),
        jnp.roll(field, -2, 1),
        lattice[1],
    )
    return -(flux_x + flux_y)


def swap(cells):
    return lax.ppermute(cells, "vert", [(0, 1), (1, 0)])


SUBSTEPS = (
    (5.0 / 48.0, 0.0, -1.0 / 48.0, 0.0, 1.0, step_half, 0.0, 0.0),
    (1.0 / 6.0, -1.0 / 3.0, -1.0 / 12.0, 2.0 / 3.0, 1.0, step_half, 0.0, 0.0),
    (-1.0 / 48.0, -1.0 / 12.0, 5.0 / 48.0, -7.0 / 12.0, 0.0, 0.0, 1.0, 0.0),
    (0.0, 0.0, 0.0, 0.0, 1.0, step_half, 0.0, 1.0),
)


def general(start_field, start_collision, mine, other, lattice):
    table = jnp.array(SUBSTEPS, jnp.float32)

    def substep(index, state):
        field, rounded, third, fourth = state
        weight = lax.dynamic_index_in_dim(table, index, 0, keepdims=False)
        drift = transport(field, lattice)
        change = field - rounded
        third = third + weight[0] * drift + weight[1] * change
        fourth = fourth + weight[2] * drift + weight[3] * change
        value = weight[4] * field + weight[5] * drift + weight[6] * third + weight[7] * fourth
        rounded = lax.reduce_precision(value, 8, 7)
        narrow = rounded.astype(jnp.bfloat16)
        field = jnp.einsum("xyw,vw->xyv", narrow, mine, preferred_element_type=jnp.float32) + jnp.einsum(
            "xyw,vw->xyv", swap(narrow), other, preferred_element_type=jnp.float32
        )
        return field, rounded, third, fourth

    third = start_field + (5.0 / 48.0) * start_collision
    fourth = (-1.0 / 48.0) * start_collision
    field, rounded, _, _ = lax.fori_loop(0, len(SUBSTEPS), substep, (start_field, start_field, third, fourth))
    return field, (field - rounded) * (1.0 / step_half)


def call(body, outs, cost, meta, operands, scratch=()):
    return pl.pallas_call(
        body,
        out_shape=outs,
        in_specs=[pl.BlockSpec(memory_space=pltpu.SMEM)] + [pl.BlockSpec(memory_space=pltpu.VMEM)] * len(operands),
        out_specs=[
            pl.BlockSpec(memory_space=pltpu.SMEM if out.shape == (1,) else pltpu.VMEM) for out in outs
        ],
        scratch_shapes=list(scratch),
        compiler_params=pltpu.CompilerParams(vmem_limit_bytes=16 * MIB),
        cost_estimate=pl.CostEstimate(flops=cost[0], bytes_accessed=cost[1], transcendentals=0),
    )(meta, *operands)


TILE = 256


def product(left, right):
    return lax.dot_general(left, right, (((1,), (0,)), ((), ())), preferred_element_type=jnp.float32)


def product_t(left, right):
    return lax.dot_general(left, right, (((1,), (1,)), ((), ())), preferred_element_type=jnp.float32)


def places(row):
    width = row.shape[1]
    tiles = width // LANES
    value = row.astype(jnp.float32)
    kinds = [value > 0.0, value < 0.0, value == 0.0]
    parts = [
        jnp.where(kind[:, t * LANES : (t + 1) * LANES], 1.0, 0.0) for kind in kinds for t in range(tiles)
    ]
    stacked = jnp.concatenate(parts, axis=0)
    down = lax.broadcasted_iota(jnp.int32, (LANES, LANES), 0)
    along = lax.broadcasted_iota(jnp.int32, (LANES, LANES), 1)
    within = product(stacked, jnp.where(down < along, 1.0, 0.0))
    totals = product(stacked, jnp.ones((LANES, LANES), jnp.float32))
    ranks, sums = [], []
    for kind in range(3):
        base = jnp.zeros((1, LANES), jnp.float32)
        row_ranks = []
        for t in range(tiles):
            at = kind * tiles + t
            row_ranks.append(within[at : at + 1] + base)
            base = base + totals[at : at + 1]
        ranks.append(row_ranks)
        sums.append(base)
    spots = []
    for t in range(tiles):
        at = slice(t * LANES, (t + 1) * LANES)
        spots.append(
            jnp.where(
                kinds[0][:, at],
                ranks[0][t],
                jnp.where(kinds[1][:, at], width - sums[1] + ranks[1][t], sums[0] + ranks[2][t]),
            )
        )
    return jnp.concatenate(spots, axis=1), jnp.maximum(sums[0], sums[1])


def one_hot(spots, low, count):
    width = spots.shape[1]
    down = lax.broadcasted_iota(jnp.int32, (count, width), 0) + low
    return jnp.where(spots.astype(jnp.int32) == down, 1.0, 0.0).astype(jnp.bfloat16)


def each_tile(width):
    def run(body):
        for low in range(0, width, TILE):
            body(low)

    return run


def put_halo(tail, head, value, low):
    rows, _, span = value.shape
    cap = tail.shape[2]
    count = min(cap - low, span)
    if count > 0:
        tail[:, :, pl.ds(low, count)] = value[rows - 2 :, :, :count]
    start = low - head_lane(cap)
    skip = max(-start, 0)
    if skip < span:
        head[:, :, pl.ds(start + skip, span - skip)] = value[:2, :, skip:]


def head_lane(cap):
    return cap // 5 * 3


def sort_body(meta, lattice, start, *refs):
    hot, main, most, to_next, to_last, spots_at = refs
    rows, cells, width = start.shape
    spots, larger = places(lattice[0:1, :])
    most[...] = jnp.broadcast_to(larger, most.shape)
    spots_at[...] = jnp.broadcast_to(spots, spots_at.shape)
    narrow = start[...].astype(jnp.bfloat16).reshape(rows * cells, width)

    @each_tile(width)
    def _(low):
        some = one_hot(spots_at[0:1, :], low, TILE)
        at = pl.ds(low, TILE)
        hot[at, :] = some
        value = product_t(narrow, some).astype(jnp.bfloat16).reshape(rows, cells, TILE)
        main[:, :, at] = value
        put_halo(to_next, to_last, value, low)


def weights_body(meta, hot, lattice, weights):
    del meta
    both = lattice[...].astype(jnp.float32).astype(jnp.bfloat16)
    sorted_both = product_t(both, hot[...])
    speed = jnp.abs(sorted_both) * lattice_speed
    weights[0:1, :] = -1.5 * (speed[0:1] + speed[1:2])
    weights[1:2, :] = 2.0 * speed[0:1]
    weights[2:3, :] = -0.5 * speed[0:1]
    weights[3:4, :] = 2.0 * speed[1:2]
    weights[4:5, :] = -0.5 * speed[1:2]
    weights[5:7, :] = sorted_both
    weights[7:8, :] = jnp.zeros_like(speed[0:1])


def rest_body(meta, collision, hot, token, out):
    del meta, token
    rows, cells, width = collision.shape
    narrow = collision[...].astype(jnp.bfloat16).reshape(rows * cells, width)

    @each_tile(width)
    def _(low):
        at = pl.ds(low, TILE)
        out[:, :, at] = product_t(narrow, hot[at, :]).astype(jnp.bfloat16).reshape(rows, cells, TILE)


def inverse_body(meta, lattice, most, inverse, hot, own_last, other_last, own, other, token, crowded, hot_other, spots_at):
    width = hot.shape[0]
    spots, larger = places(lattice[0:1, :])
    largest = jnp.maximum(most[...], larger)
    token[...] = largest
    crowded[0] = (jnp.max(largest) > float(width // 8 * 5)).astype(jnp.int32)
    spots_at[...] = jnp.broadcast_to(spots, spots_at.shape)

    @each_tile(width)
    def _(low):
        hot_other[pl.ds(low, TILE), :] = one_hot(spots_at[0:1, :], low, TILE)

    for source, last, final, place in (
        (hot, own_last, own, meta[0]),
        (hot_other, other_last, other, 1 - meta[0]),
    ):
        columns = pl.ds(pl.multiple_of(place * width, width), width)

        for low in range(0, width, TILE):
            at = pl.ds(low, TILE)
            value = product_t(source[at, :], inverse[:, columns]).astype(jnp.bfloat16)
            last[at, :] = value
            for far in range(0, width, TILE):
                to = pl.ds(far, TILE)
                final[at, to] = product_t(value, hot[to, :]).astype(jnp.bfloat16)


def drift_at(row, at, region, refs, left, right):
    field, before, after, weights = refs
    rows, size, _ = field.shape
    centre = field[row, :, at]

    def behind(step):
        source = row - step
        if source >= 0:
            return field[source, :, at].astype(jnp.float32)
        return left[2 + source]

    def ahead(step):
        source = row + step
        if source < rows:
            return field[source, :, at].astype(jnp.float32)
        return right[source - rows]

    def one(step):
        if region == 0:
            return behind(step)
        if region == 2:
            return ahead(step)
        return jnp.where(weights[5:6, at] > 0.0, behind(step), ahead(step))

    long = jnp.concatenate(
        [
            before[row, before.shape[1] - EDGE :, at].astype(jnp.float32),
            centre.astype(jnp.float32),
            after[row, 0:EDGE, at].astype(jnp.float32),
        ],
        axis=0,
    )
    centre = centre.astype(jnp.float32)
    up = weights[6:7, at] > 0.0

    def beside(step):
        return jnp.where(up, long[EDGE - step : EDGE - step + size], long[EDGE + step : EDGE + step + size])

    total = weights[0:1, at] * centre
    total = total + weights[1:2, at] * one(1) + weights[2:3, at] * one(2)
    total = total + weights[3:4, at] * beside(1) + weights[4:5, at] * beside(2)
    return centre, total


def drifts(fields, refs, body):
    weights, from_last, from_next = refs[:3]
    rows, _, width = fields[0].shape
    cap = from_last.shape[2]
    low = width - cap
    ends = (0, (width - cap) // LANES, cap // LANES, width // LANES)
    for region in range(3):

        for index in range(ends[region], ends[region + 1]):
            at = pl.ds(index * LANES, LANES)
            left, right = None, None
            if region < 2:
                left = [from_last[i, :, at].astype(jnp.float32) for i in range(2)]
            if region > 0:
                beyond = pl.ds(index * LANES - low, LANES)
                right = [from_next[i, :, beyond].astype(jnp.float32) for i in range(2)]
            for row in range(rows):
                body((row, slice(None), at), *drift_at(row, at, region, (*fields, weights), left, right))


def part(ref, index):
    size = ref.shape[1] // CHUNKS
    return ref.at[:, pl.ds(index % CHUNKS * size, size), :]


def stage_one(index):
    def kernel(meta, start, *refs):
        del meta
        weights, from_last, from_next, _, rounded, drift = refs
        around = weights, part(from_last, index), part(from_next, index)

        def body(at, centre, total):
            drift[at] = total
            rounded[at] = (centre + step_half * total).astype(jnp.bfloat16)

        drifts((part(start, index), part(start, index - 1), part(start, index + 1)), around, body)

    return kernel


def stage_two(index):
    def kernel(meta, field, before, after, *refs):
        del meta
        start, collision, drift, rounded_one, rounded, part_one, part_two = refs[3:]
        start, collision = part(start, index), part(collision, index)

        def body(at, centre, total):
            rounded[at] = (centre + step_half * total).astype(jnp.bfloat16)
            change = centre - rounded_one[at].astype(jnp.float32)
            zero = drift[at] + collision[at].astype(jnp.float32)
            base = start[at].astype(jnp.float32)
            part_one[at] = base + (5.0 / 48.0) * zero + (1.0 / 6.0) * total - (1.0 / 3.0) * change
            part_two[at] = (2.0 / 3.0) * change - (1.0 / 48.0) * zero - (1.0 / 12.0) * total

        drifts((field, before, after), refs, body)

    return kernel


def stage_three(index):
    del index

    def kernel(meta, field, before, after, *refs):
        del meta
        rounded_two, part_one, part_two, rounded, rest = refs[3:]

        def body(at, centre, total):
            change = centre - rounded_two[at].astype(jnp.float32)
            rounded[at] = (part_one[at] - (1.0 / 48.0) * total - (1.0 / 12.0) * change).astype(jnp.bfloat16)
            rest[at] = part_two[at] + (5.0 / 48.0) * total - (7.0 / 12.0) * change

        drifts((field, before, after), refs, body)

    return kernel


def stage_four(index):
    del index

    def kernel(meta, field, before, after, *refs):
        del meta
        rest, rounded = refs[3:]

        def body(at, centre, total):
            rounded[at] = (centre + step_half * total + rest[at]).astype(jnp.bfloat16)

        drifts((field, before, after), refs, body)

    return kernel


def collide_body(meta, mine, beside, own, other, field, to_next, to_last, token):
    del meta
    rows, size, width = field.shape

    @each_tile(width)
    def _(low):
        at = pl.ds(low, TILE)
        first = mine[...].reshape(rows * size, width)
        second = beside[...].reshape(rows * size, width)
        result = (product(first, own[:, at]) + product(second, other[:, at])).reshape(rows, size, TILE)
        field[:, :, at] = result
        put_halo(to_next, to_last, result.astype(jnp.bfloat16), low)

    token[...] = jnp.zeros_like(token)


def unsort_body(meta, rounded, hot, plain):
    del meta
    rows, size, width = rounded.shape
    first = rounded[...].reshape(rows * size, width)

    @each_tile(width)
    def _(low):
        at = pl.ds(low, TILE)
        plain[:, :, at] = product(first, hot[:, at]).astype(jnp.bfloat16).reshape(rows, size, TILE)


def last_body(*refs):
    mine, beside, plain = refs[:CHUNKS], refs[CHUNKS : 2 * CHUNKS], refs[2 * CHUNKS : 3 * CHUNKS]
    own, other, field, collision = refs[3 * CHUNKS :]
    at = pl.ds(pl.multiple_of(pl.program_id(0) * TILE, TILE), TILE)
    for index in range(CHUNKS):
        rows, size, width = mine[index].shape
        first = mine[index][...].reshape(rows * size, width)
        second = beside[index][...].reshape(rows * size, width)
        result = (product(first, own[:, at]) + product(second, other[:, at])).reshape(rows, size, TILE)
        ys = pl.ds(index * size, size)
        field[:, ys, :] = result
        collision[:, ys, :] = (result - plain[index][:, :, at].astype(jnp.float32)) * (1.0 / step_half)


def sorted_path(cap, start_field, start_collision, inverse, lattice):
    rows, cells, width = start_field.shape
    size = cells // CHUNKS
    count = lax.axis_size("gx")
    forth = [(i, (i + 1) % count) for i in range(count)]
    back = [((i + 1) % count, i) for i in range(count)]
    meta = lax.axis_index("vert").astype(jnp.int32).reshape(1)
    narrow = jnp.bfloat16

    def shape(dims, dtype=jnp.float32):
        return jax.ShapeDtypeStruct(dims, dtype)

    halo_shape = shape((2, size, cap), narrow)
    square = shape((width, width), narrow)
    wide_shape = shape((rows, size, width))
    thin_shape = shape((rows, size, width), narrow)
    token_shape = shape((8, LANES))
    elements = rows * size * width

    def exchange(to_next, to_last):
        return lax.ppermute(to_next, "gx", forth), lax.ppermute(to_last, "gx", back)

    beside_lattice = swap(lattice)
    hot, main, most, *ends = call(
        sort_body,
        [square, shape((rows, cells, width), narrow), token_shape] + [shape((2, cells, cap), narrow)] * 2,
        (4 * elements * width, 16 * elements),
        meta,
        (lattice, start_field),
        [pltpu.VMEM((8, width), jnp.float32)],
    )
    halos = [exchange(*ends)] * CHUNKS
    (weights,) = call(weights_body, [shape((8, width))], (1, 1), meta, (hot, lattice))
    own_last, other_last, own, other, largest, crowded = call(
        inverse_body,
        [square] * 4 + [token_shape, shape((1,), jnp.int32)],
        (8 * width**3, 20 * width**2),
        meta,
        (beside_lattice, most, inverse, hot),
        [pltpu.VMEM((width, width), narrow), pltpu.VMEM((8, width), jnp.float32)],
    )

    def stage(body, outs, fields, index, *extra):
        return call(
            body(index),
            outs,
            (30 * elements, 16 * elements),
            meta,
            (*fields, weights, *halos[index], *extra),
        )

    def advance(rounded):
        results = [
            call(
                collide_body,
                [wide_shape, halo_shape, halo_shape, token_shape],
                (4 * elements * width, 8 * elements + 4 * width * width),
                meta,
                (r, swap(r), own, other),
            )
            for r in rounded
        ]
        return [r[0] for r in results], [exchange(r[1], r[2]) for r in results], results[-1][3]

    def around(index):
        return fields[index], fields[index - 1], fields[(index + 1) % CHUNKS]

    every = range(CHUNKS)
    kept = [stage(stage_one, [thin_shape, wide_shape], (main,), i, largest) for i in every]
    fields, halos, token = advance([k[0] for k in kept])
    (collision,) = call(
        rest_body,
        [shape((rows, cells, width), narrow)],
        (2 * CHUNKS * elements * width, 6 * CHUNKS * elements),
        meta,
        (start_collision, hot, token),
    )
    kept = [
        stage(
            stage_two, [thin_shape, wide_shape, wide_shape], around(i), i, main, collision, kept[i][1], kept[i][0]
        )
        for i in every
    ]
    fields, halos, token = advance([k[0] for k in kept])
    kept = [stage(stage_three, [thin_shape, wide_shape], around(i), i, *kept[i]) for i in every]
    fields, halos, token = advance([k[0] for k in kept])
    rounded = [stage(stage_four, [thin_shape], around(i), i, kept[i][1])[0] for i in every]
    beside = [swap(r) for r in rounded]
    plain = [
        call(unsort_body, [thin_shape], (2 * elements * width, 4 * elements), meta, (r, hot))[0] for r in rounded
    ]
    operands = (*rounded, *beside, *plain, own_last, other_last)
    ends = pl.pallas_call(
        last_body,
        grid=(width // TILE,),
        out_shape=[shape((rows, cells, width))] * 2,
        in_specs=[pl.BlockSpec(memory_space=pltpu.VMEM)] * len(operands),
        out_specs=[pl.BlockSpec((rows, cells, TILE), lambda i: (0, 0, i))] * 2,
        compiler_params=pltpu.CompilerParams(vmem_limit_bytes=16 * MIB),
        cost_estimate=pl.CostEstimate(
            flops=4 * CHUNKS * elements * width, bytes_accessed=12 * CHUNKS * elements, transcendentals=0
        ),
    )(*operands)
    return (*ends, crowded)


def per_device(start_field, start_collision, inverse, lattice):
    width = start_field.shape[2]
    cap = width // 8 * 5
    field, collision, crowded = sorted_path(cap, start_field, start_collision, inverse, lattice)

    def again(state):
        here = lax.axis_index("vert")
        mine = lax.dynamic_slice_in_dim(inverse, here * width, width, axis=1)
        other = lax.dynamic_slice_in_dim(inverse, (1 - here) * width, width, axis=1)
        return (*general(start_field, start_collision, mine, other, lattice), jnp.zeros((1,), jnp.int32))

    field, collision, _ = lax.while_loop(lambda state: state[2][0] > 0, again, (field, collision, crowded))
    return field, collision


def solution(mesh):
    return jax.shard_map(
        per_device,
        mesh=mesh,
        in_specs=(P("gx", None, "vert"), P("gx", None, "vert"), P("vert", None), P(None, "vert")),
        out_specs=(P("gx", None, "vert"), P("gx", None, "vert")),
        check_vma=False,
    )
```

```python
import jax
import jax.numpy as jnp
from jax import lax
from jax.experimental import pallas as pl
from jax.experimental.pallas import tpu as pltpu
from jax.sharding import PartitionSpec as P

CHUNKS = 2

step_half = 0.25
lattice_speed = 0.07

LANES = 128
EDGE = 8
MIB = 1 << 20


def padded_2(cells, axis):
    count = lax.axis_size(axis)
    head = cells[:2].astype(jnp.bfloat16)
    tail = cells[-2:].astype(jnp.bfloat16)
    return jnp.concatenate(
        [
            lax.ppermute(tail, axis, [(i, (i + 1) % count) for i in range(count)]).astype(cells.dtype),
            cells,
            lax.ppermute(head, axis, [((i + 1) % count, i) for i in range(count)]).astype(cells.dtype),
        ],
        axis=0,
    )


def upwind(minus_two, minus_one, centre, plus_one, plus_two, lattice_row):
    speed = lattice_row.astype(jnp.float32) * lattice_speed
    backward = 1.5 * centre - 2.0 * minus_one + 0.5 * minus_two
    forward = -1.5 * centre + 2.0 * plus_one - 0.5 * plus_two
    return jnp.where(lattice_row > 0, speed * backward, speed * forward)


def transport(field, lattice):
    padded = padded_2(field, "gx")
    rows = field.shape[0]
    flux_x = upwind(
        padded[0:rows],
        padded[1 : rows + 1],
        field,
        padded[3 : rows + 3],
        padded[4 : rows + 4],
        lattice[0],
    )
    flux_y = upwind(
        jnp.roll(field, 2, 1),
        jnp.roll(field, 1, 1),
        field,
        jnp.roll(field, -1, 1),
        jnp.roll(field, -2, 1),
        lattice[1],
    )
    return -(flux_x + flux_y)


def swap(cells):
    return lax.ppermute(cells, "vert", [(0, 1), (1, 0)])


SUBSTEPS = (
    (5.0 / 48.0, 0.0, -1.0 / 48.0, 0.0, 1.0, step_half, 0.0, 0.0),
    (1.0 / 6.0, -1.0 / 3.0, -1.0 / 12.0, 2.0 / 3.0, 1.0, step_half, 0.0, 0.0),
    (-1.0 / 48.0, -1.0 / 12.0, 5.0 / 48.0, -7.0 / 12.0, 0.0, 0.0, 1.0, 0.0),
    (0.0, 0.0, 0.0, 0.0, 1.0, step_half, 0.0, 1.0),
)


def general(start_field, start_collision, mine, other, lattice):
    table = jnp.array(SUBSTEPS, jnp.float32)

    def substep(index, state):
        field, rounded, third, fourth = state
        weight = lax.dynamic_index_in_dim(table, index, 0, keepdims=False)
        drift = transport(field, lattice)
        change = field - rounded
        third = third + weight[0] * drift + weight[1] * change
        fourth = fourth + weight[2] * drift + weight[3] * change
        value = weight[4] * field + weight[5] * drift + weight[6] * third + weight[7] * fourth
        rounded = lax.reduce_precision(value, 8, 7)
        narrow = rounded.astype(jnp.bfloat16)
        field = jnp.einsum("xyw,vw->xyv", narrow, mine, preferred_element_type=jnp.float32) + jnp.einsum(
            "xyw,vw->xyv", swap(narrow), other, preferred_element_type=jnp.float32
        )
        return field, rounded, third, fourth

    third = start_field + (5.0 / 48.0) * start_collision
    fourth = (-1.0 / 48.0) * start_collision
    field, rounded, _, _ = lax.fori_loop(0, len(SUBSTEPS), substep, (start_field, start_field, third, fourth))
    return field, (field - rounded) * (1.0 / step_half)


def call(body, outs, cost, meta, operands, scratch=()):
    return pl.pallas_call(
        body,
        out_shape=outs,
        in_specs=[pl.BlockSpec(memory_space=pltpu.SMEM)] + [pl.BlockSpec(memory_space=pltpu.VMEM)] * len(operands),
        out_specs=[
            pl.BlockSpec(memory_space=pltpu.SMEM if out.shape == (1,) else pltpu.VMEM) for out in outs
        ],
        scratch_shapes=list(scratch),
        compiler_params=pltpu.CompilerParams(vmem_limit_bytes=16 * MIB),
        cost_estimate=pl.CostEstimate(flops=cost[0], bytes_accessed=cost[1], transcendentals=0),
    )(meta, *operands)


TILE = 256


def product(left, right):
    return lax.dot_general(left, right, (((1,), (0,)), ((), ())), preferred_element_type=jnp.float32)


def product_t(left, right):
    return lax.dot_general(left, right, (((1,), (1,)), ((), ())), preferred_element_type=jnp.float32)


def places(row):
    width = row.shape[1]
    tiles = width // LANES
    value = row.astype(jnp.float32)
    kinds = [value > 0.0, value < 0.0, value == 0.0]
    parts = [
        jnp.where(kind[:, t * LANES : (t + 1) * LANES], 1.0, 0.0) for kind in kinds for t in range(tiles)
    ]
    stacked = jnp.concatenate(parts, axis=0)
    down = lax.broadcasted_iota(jnp.int32, (LANES, LANES), 0)
    along = lax.broadcasted_iota(jnp.int32, (LANES, LANES), 1)
    within = product(stacked, jnp.where(down < along, 1.0, 0.0))
    totals = product(stacked, jnp.ones((LANES, LANES), jnp.float32))
    ranks, sums = [], []
    for kind in range(3):
        base = jnp.zeros((1, LANES), jnp.float32)
        row_ranks = []
        for t in range(tiles):
            at = kind * tiles + t
            row_ranks.append(within[at : at + 1] + base)
            base = base + totals[at : at + 1]
        ranks.append(row_ranks)
        sums.append(base)
    spots = []
    for t in range(tiles):
        at = slice(t * LANES, (t + 1) * LANES)
        spots.append(
            jnp.where(
                kinds[0][:, at],
                ranks[0][t],
                jnp.where(kinds[1][:, at], width - sums[1] + ranks[1][t], sums[0] + ranks[2][t]),
            )
        )
    return jnp.concatenate(spots, axis=1), jnp.maximum(sums[0], sums[1])


def one_hot(spots, low, count):
    width = spots.shape[1]
    down = lax.broadcasted_iota(jnp.int32, (count, width), 0) + low
    return jnp.where(spots.astype(jnp.int32) == down, 1.0, 0.0).astype(jnp.bfloat16)


def each_tile(width):
    def run(body):
        for low in range(0, width, TILE):
            body(low)

    return run


def put_halo(tail, head, value, low):
    rows, _, span = value.shape
    cap = tail.shape[2]
    count = min(cap - low, span)
    if count > 0:
        tail[:, :, pl.ds(low, count)] = value[rows - 2 :, :, :count]
    start = low - head_lane(cap)
    skip = max(-start, 0)
    if skip < span:
        head[:, :, pl.ds(start + skip, span - skip)] = value[:2, :, skip:]


def head_lane(cap):
    return cap // 5 * 3


def sort_body(meta, lattice, start, *refs):
    hot, main, most, to_next, to_last, spots_at = refs
    rows, cells, width = start.shape
    spots, larger = places(lattice[0:1, :])
    most[...] = jnp.broadcast_to(larger, most.shape)
    spots_at[...] = jnp.broadcast_to(spots, spots_at.shape)
    narrow = start[...].astype(jnp.bfloat16).reshape(rows * cells, width)

    @each_tile(width)
    def _(low):
        some = one_hot(spots_at[0:1, :], low, TILE)
        at = pl.ds(low, TILE)
        hot[at, :] = some
        value = product_t(narrow, some).astype(jnp.bfloat16).reshape(rows, cells, TILE)
        main[:, :, at] = value
        put_halo(to_next, to_last, value, low)


def weights_body(meta, hot, lattice, weights):
    del meta
    both = lattice[...].astype(jnp.float32).astype(jnp.bfloat16)
    sorted_both = product_t(both, hot[...])
    speed = jnp.abs(sorted_both) * lattice_speed
    weights[0:1, :] = -1.5 * (speed[0:1] + speed[1:2])
    weights[1:2, :] = 2.0 * speed[0:1]
    weights[2:3, :] = -0.5 * speed[0:1]
    weights[3:4, :] = 2.0 * speed[1:2]
    weights[4:5, :] = -0.5 * speed[1:2]
    weights[5:7, :] = sorted_both
    weights[7:8, :] = jnp.zeros_like(speed[0:1])


def rest_body(meta, collision, hot, token, out):
    del meta, token
    rows, cells, width = collision.shape
    narrow = collision[...].astype(jnp.bfloat16).reshape(rows * cells, width)

    @each_tile(width)
    def _(low):
        at = pl.ds(low, TILE)
        out[:, :, at] = product_t(narrow, hot[at, :]).astype(jnp.bfloat16).reshape(rows, cells, TILE)


def inverse_body(meta, lattice, most, inverse, hot, own_last, other_last, own, other, token, crowded, hot_other, spots_at):
    width = hot.shape[0]
    spots, larger = places(lattice[0:1, :])
    largest = jnp.maximum(most[...], larger)
    token[...] = largest
    crowded[0] = (jnp.max(largest) > float(width // 8 * 5)).astype(jnp.int32)
    spots_at[...] = jnp.broadcast_to(spots, spots_at.shape)

    @each_tile(width)
    def _(low):
        hot_other[pl.ds(low, TILE), :] = one_hot(spots_at[0:1, :], low, TILE)

    for source, last, final, place in (
        (hot, own_last, own, meta[0]),
        (hot_other, other_last, other, 1 - meta[0]),
    ):
        columns = pl.ds(pl.multiple_of(place * width, width), width)

        for low in range(0, width, TILE):
            at = pl.ds(low, TILE)
            value = product_t(source[at, :], inverse[:, columns]).astype(jnp.bfloat16)
            last[at, :] = value
            for far in range(0, width, TILE):
                to = pl.ds(far, TILE)
                final[at, to] = product_t(value, hot[to, :]).astype(jnp.bfloat16)


def drift_at(row, at, region, refs, left, right):
    field, before, after, weights = refs
    rows, size, _ = field.shape
    centre = field[row, :, at]

    def behind(step):
        source = row - step
        if source >= 0:
            return field[source, :, at].astype(jnp.float32)
        return left[2 + source]

    def ahead(step):
        source = row + step
        if source < rows:
            return field[source, :, at].astype(jnp.float32)
        return right[source - rows]

    def one(step):
        if region == 0:
            return behind(step)
        if region == 2:
            return ahead(step)
        return jnp.where(weights[5:6, at] > 0.0, behind(step), ahead(step))

    long = jnp.concatenate(
        [
            before[row, before.shape[1] - EDGE :, at].astype(jnp.float32),
            centre.astype(jnp.float32),
            after[row, 0:EDGE, at].astype(jnp.float32),
        ],
        axis=0,
    )
    centre = centre.astype(jnp.float32)
    up = weights[6:7, at] > 0.0

    def beside(step):
        return jnp.where(up, long[EDGE - step : EDGE - step + size], long[EDGE + step : EDGE + step + size])

    total = weights[0:1, at] * centre
    total = total + weights[1:2, at] * one(1) + weights[2:3, at] * one(2)
    total = total + weights[3:4, at] * beside(1) + weights[4:5, at] * beside(2)
    return centre, total


def drifts(fields, refs, body):
    weights, from_last, from_next = refs[:3]
    rows, _, width = fields[0].shape
    cap = from_last.shape[2]
    low = width - cap
    ends = (0, (width - cap) // LANES, cap // LANES, width // LANES)
    for region in range(3):

        for index in range(ends[region], ends[region + 1]):
            at = pl.ds(index * LANES, LANES)
            left, right = None, None
            if region < 2:
                left = [from_last[i, :, at].astype(jnp.float32) for i in range(2)]
            if region > 0:
                beyond = pl.ds(index * LANES - low, LANES)
                right = [from_next[i, :, beyond].astype(jnp.float32) for i in range(2)]
            for row in range(rows):
                body((row, slice(None), at), *drift_at(row, at, region, (*fields, weights), left, right))


def part(ref, index):
    size = ref.shape[1] // CHUNKS
    return ref.at[:, pl.ds(index % CHUNKS * size, size), :]


def stage_one(index):
    def kernel(meta, start, *refs):
        del meta
        weights, from_last, from_next, _, rounded, drift = refs
        around = weights, part(from_last, index), part(from_next, index)

        def body(at, centre, total):
            drift[at] = total
            rounded[at] = (centre + step_half * total).astype(jnp.bfloat16)

        drifts((part(start, index), part(start, index - 1), part(start, index + 1)), around, body)

    return kernel


def stage_two(index):
    def kernel(meta, field, before, after, *refs):
        del meta
        start, collision, drift, rounded_one, rounded, part_one, part_two = refs[3:]
        start, collision = part(start, index), part(collision, index)

        def body(at, centre, total):
            rounded[at] = (centre + step_half * total).astype(jnp.bfloat16)
            change = centre - rounded_one[at].astype(jnp.float32)
            zero = drift[at] + collision[at].astype(jnp.float32)
            base = start[at].astype(jnp.float32)
            part_one[at] = base + (5.0 / 48.0) * zero + (1.0 / 6.0) * total - (1.0 / 3.0) * change
            part_two[at] = (2.0 / 3.0) * change - (1.0 / 48.0) * zero - (1.0 / 12.0) * total

        drifts((field, before, after), refs, body)

    return kernel


def stage_three(index):
    del index

    def kernel(meta, field, before, after, *refs):
        del meta
        rounded_two, part_one, part_two, rounded, rest = refs[3:]

        def body(at, centre, total):
            change = centre - rounded_two[at].astype(jnp.float32)
            rounded[at] = (part_one[at] - (1.0 / 48.0) * total - (1.0 / 12.0) * change).astype(jnp.bfloat16)
            rest[at] = part_two[at] + (5.0 / 48.0) * total - (7.0 / 12.0) * change

        drifts((field, before, after), refs, body)

    return kernel


def stage_four(index):
    del index

    def kernel(meta, field, before, after, *refs):
        del meta
        rest, rounded = refs[3:]

        def body(at, centre, total):
            rounded[at] = (centre + step_half * total + rest[at]).astype(jnp.bfloat16)

        drifts((field, before, after), refs, body)

    return kernel


def collide_body(meta, mine, beside, own, other, field, to_next, to_last, token):
    del meta
    rows, size, width = field.shape

    @each_tile(width)
    def _(low):
        at = pl.ds(low, TILE)
        first = mine[...].reshape(rows * size, width)
        second = beside[...].reshape(rows * size, width)
        result = (product(first, own[:, at]) + product(second, other[:, at])).reshape(rows, size, TILE)
        field[:, :, at] = result
        put_halo(to_next, to_last, result.astype(jnp.bfloat16), low)

    token[...] = jnp.zeros_like(token)


def unsort_body(meta, rounded, hot, plain):
    del meta
    rows, size, width = rounded.shape
    first = rounded[...].reshape(rows * size, width)

    @each_tile(width)
    def _(low):
        at = pl.ds(low, TILE)
        plain[:, :, at] = product(first, hot[:, at]).astype(jnp.bfloat16).reshape(rows, size, TILE)


def last_body(*refs):
    mine, beside, plain = refs[:CHUNKS], refs[CHUNKS : 2 * CHUNKS], refs[2 * CHUNKS : 3 * CHUNKS]
    own, other, field, collision = refs[3 * CHUNKS :]
    at = pl.ds(pl.multiple_of(pl.program_id(0) * TILE, TILE), TILE)
    for index in range(CHUNKS):
        rows, size, width = mine[index].shape
        first = mine[index][...].reshape(rows * size, width)
        second = beside[index][...].reshape(rows * size, width)
        result = (product(first, own[:, at]) + product(second, other[:, at])).reshape(rows, size, TILE)
        ys = pl.ds(index * size, size)
        field[:, ys, :] = result
        collision[:, ys, :] = (result - plain[index][:, :, at].astype(jnp.float32)) * (1.0 / step_half)


def sorted_path(cap, start_field, start_collision, inverse, lattice):
    rows, cells, width = start_field.shape
    size = cells // CHUNKS
    count = lax.axis_size("gx")
    forth = [(i, (i + 1) % count) for i in range(count)]
    back = [((i + 1) % count, i) for i in range(count)]
    meta = lax.axis_index("vert").astype(jnp.int32).reshape(1)
    narrow = jnp.bfloat16

    def shape(dims, dtype=jnp.float32):
        return jax.ShapeDtypeStruct(dims, dtype)

    halo_shape = shape((2, size, cap), narrow)
    square = shape((width, width), narrow)
    wide_shape = shape((rows, size, width))
    thin_shape = shape((rows, size, width), narrow)
    token_shape = shape((8, LANES))
    elements = rows * size * width

    def exchange(to_next, to_last, turn=0):
        if turn % 2:
            from_next = lax.ppermute(to_last, "gx", back)
            return lax.ppermute(to_next, "gx", forth), from_next
        from_last = lax.ppermute(to_next, "gx", forth)
        return from_last, lax.ppermute(to_last, "gx", back)

    beside_lattice = swap(lattice)
    hot, main, most, *ends = call(
        sort_body,
        [square, shape((rows, cells, width), narrow), token_shape] + [shape((2, cells, cap), narrow)] * 2,
        (4 * elements * width, 16 * elements),
        meta,
        (lattice, start_field),
        [pltpu.VMEM((8, width), jnp.float32)],
    )
    halos = [exchange(*ends)] * CHUNKS
    (weights,) = call(weights_body, [shape((8, width))], (1, 1), meta, (hot, lattice))
    own_last, other_last, own, other, largest, crowded = call(
        inverse_body,
        [square] * 4 + [token_shape, shape((1,), jnp.int32)],
        (8 * width**3, 20 * width**2),
        meta,
        (beside_lattice, most, inverse, hot),
        [pltpu.VMEM((width, width), narrow), pltpu.VMEM((8, width), jnp.float32)],
    )

    def stage(body, outs, fields, index, *extra):
        kernel = body(index)
        place = 1 + len(fields)
        if index % 2:

            def ordered(meta, *refs):
                refs = list(refs)
                refs[place], refs[place + 1] = refs[place + 1], refs[place]
                kernel(meta, *refs)

        else:
            ordered = kernel
        return call(
            ordered,
            outs,
            (30 * elements, 16 * elements),
            meta,
            (*fields, weights, *halos[index][:: -1 if index % 2 else 1], *extra),
        )

    def advance(rounded):
        results = [
            call(
                collide_body,
                [wide_shape, halo_shape, halo_shape, token_shape],
                (4 * elements * width, 8 * elements + 4 * width * width),
                meta,
                (r, swap(r), own, other),
            )
            for r in rounded
        ]
        return [r[0] for r in results], [exchange(r[1], r[2], turn) for turn, r in enumerate(results)], results[-1][3]

    def around(index):
        return fields[index], fields[index - 1], fields[(index + 1) % CHUNKS]

    every = range(CHUNKS)
    kept = [stage(stage_one, [thin_shape, wide_shape], (main,), i, largest) for i in every]
    fields, halos, token = advance([k[0] for k in kept])
    (collision,) = call(
        rest_body,
        [shape((rows, cells, width), narrow)],
        (2 * CHUNKS * elements * width, 6 * CHUNKS * elements),
        meta,
        (start_collision, hot, token),
    )
    kept = [
        stage(
            stage_two, [thin_shape, wide_shape, wide_shape], around(i), i, main, collision, kept[i][1], kept[i][0]
        )
        for i in every
    ]
    fields, halos, token = advance([k[0] for k in kept])
    kept = [stage(stage_three, [thin_shape, wide_shape], around(i), i, *kept[i]) for i in every]
    fields, halos, token = advance([k[0] for k in kept])
    rounded = [stage(stage_four, [thin_shape], around(i), i, kept[i][1])[0] for i in every]
    beside = [swap(r) for r in rounded]
    plain = [
        call(unsort_body, [thin_shape], (2 * elements * width, 4 * elements), meta, (r, hot))[0] for r in rounded
    ]
    operands = (*rounded, *beside, *plain, own_last, other_last)
    ends = pl.pallas_call(
        last_body,
        grid=(width // TILE,),
        out_shape=[shape((rows, cells, width))] * 2,
        in_specs=[pl.BlockSpec(memory_space=pltpu.VMEM)] * len(operands),
        out_specs=[pl.BlockSpec((rows, cells, TILE), lambda i: (0, 0, i))] * 2,
        compiler_params=pltpu.CompilerParams(vmem_limit_bytes=16 * MIB),
        cost_estimate=pl.CostEstimate(
            flops=4 * CHUNKS * elements * width, bytes_accessed=12 * CHUNKS * elements, transcendentals=0
        ),
    )(*operands)
    return (*ends, crowded)


def per_device(start_field, start_collision, inverse, lattice):
    width = start_field.shape[2]
    cap = width // 8 * 5
    field, collision, crowded = sorted_path(cap, start_field, start_collision, inverse, lattice)

    def again(state):
        here = lax.axis_index("vert")
        mine = lax.dynamic_slice_in_dim(inverse, here * width, width, axis=1)
        other = lax.dynamic_slice_in_dim(inverse, (1 - here) * width, width, axis=1)
        return (*general(start_field, start_collision, mine, other, lattice), jnp.zeros((1,), jnp.int32))

    field, collision, _ = lax.while_loop(lambda state: state[2][0] > 0, again, (field, collision, crowded))
    return field, collision


def solution(mesh):
    return jax.shard_map(
        per_device,
        mesh=mesh,
        in_specs=(P("gx", None, "vert"), P("gx", None, "vert"), P("vert", None), P(None, "vert")),
        out_specs=(P("gx", None, "vert"), P("gx", None, "vert")),
        check_vma=False,
    )
```

```python
import jax
import jax.numpy as jnp
from jax import lax
from jax.experimental import pallas as pl
from jax.experimental.pallas import tpu as pltpu
from jax.sharding import PartitionSpec as P

CHUNKS = 2

step_half = 0.25
lattice_speed = 0.07

LANES = 128
EDGE = 8
MIB = 1 << 20


def padded_2(cells, axis):
    count = lax.axis_size(axis)
    head = cells[:2].astype(jnp.bfloat16)
    tail = cells[-2:].astype(jnp.bfloat16)
    return jnp.concatenate(
        [
            lax.ppermute(tail, axis, [(i, (i + 1) % count) for i in range(count)]).astype(cells.dtype),
            cells,
            lax.ppermute(head, axis, [((i + 1) % count, i) for i in range(count)]).astype(cells.dtype),
        ],
        axis=0,
    )


def upwind(minus_two, minus_one, centre, plus_one, plus_two, lattice_row):
    speed = lattice_row.astype(jnp.float32) * lattice_speed
    backward = 1.5 * centre - 2.0 * minus_one + 0.5 * minus_two
    forward = -1.5 * centre + 2.0 * plus_one - 0.5 * plus_two
    return jnp.where(lattice_row > 0, speed * backward, speed * forward)


def transport(field, lattice):
    padded = padded_2(field, "gx")
    rows = field.shape[0]
    flux_x = upwind(
        padded[0:rows],
        padded[1 : rows + 1],
        field,
        padded[3 : rows + 3],
        padded[4 : rows + 4],
        lattice[0],
    )
    flux_y = upwind(
        jnp.roll(field, 2, 1),
        jnp.roll(field, 1, 1),
        field,
        jnp.roll(field, -1, 1),
        jnp.roll(field, -2, 1),
        lattice[1],
    )
    return -(flux_x + flux_y)


def swap(cells):
    return lax.ppermute(cells, "vert", [(0, 1), (1, 0)])


SUBSTEPS = (
    (5.0 / 48.0, 0.0, -1.0 / 48.0, 0.0, 1.0, step_half, 0.0, 0.0),
    (1.0 / 6.0, -1.0 / 3.0, -1.0 / 12.0, 2.0 / 3.0, 1.0, step_half, 0.0, 0.0),
    (-1.0 / 48.0, -1.0 / 12.0, 5.0 / 48.0, -7.0 / 12.0, 0.0, 0.0, 1.0, 0.0),
    (0.0, 0.0, 0.0, 0.0, 1.0, step_half, 0.0, 1.0),
)


def general(start_field, start_collision, mine, other, lattice):
    table = jnp.array(SUBSTEPS, jnp.float32)

    def substep(index, state):
        field, rounded, third, fourth = state
        weight = lax.dynamic_index_in_dim(table, index, 0, keepdims=False)
        drift = transport(field, lattice)
        change = field - rounded
        third = third + weight[0] * drift + weight[1] * change
        fourth = fourth + weight[2] * drift + weight[3] * change
        value = weight[4] * field + weight[5] * drift + weight[6] * third + weight[7] * fourth
        rounded = lax.reduce_precision(value, 8, 7)
        narrow = rounded.astype(jnp.bfloat16)
        field = jnp.einsum("xyw,vw->xyv", narrow, mine, preferred_element_type=jnp.float32) + jnp.einsum(
            "xyw,vw->xyv", swap(narrow), other, preferred_element_type=jnp.float32
        )
        return field, rounded, third, fourth

    third = start_field + (5.0 / 48.0) * start_collision
    fourth = (-1.0 / 48.0) * start_collision
    field, rounded, _, _ = lax.fori_loop(0, len(SUBSTEPS), substep, (start_field, start_field, third, fourth))
    return field, (field - rounded) * (1.0 / step_half)


SPARE = LANES // 2


def call(body, outs, cost, meta, operands, scratch=()):
    return pl.pallas_call(
        body,
        out_shape=outs,
        in_specs=[pl.BlockSpec(memory_space=pltpu.SMEM)] + [pl.BlockSpec(memory_space=pltpu.VMEM)] * len(operands),
        out_specs=[
            pl.BlockSpec(memory_space=pltpu.SMEM if out.shape == (1,) else pltpu.VMEM) for out in outs
        ],
        scratch_shapes=list(scratch),
        compiler_params=pltpu.CompilerParams(vmem_limit_bytes=16 * MIB),
        cost_estimate=pl.CostEstimate(flops=cost[0], bytes_accessed=cost[1], transcendentals=0),
    )(meta, *operands)


TILE = 256


def product(left, right):
    return lax.dot_general(left, right, (((1,), (0,)), ((), ())), preferred_element_type=jnp.float32)


def product_t(left, right):
    return lax.dot_general(left, right, (((1,), (1,)), ((), ())), preferred_element_type=jnp.float32)


def places(row):
    width = row.shape[1]
    tiles = width // LANES
    value = row.astype(jnp.float32)
    kinds = [value > 0.0, value < 0.0, value == 0.0]
    parts = [
        jnp.where(kind[:, t * LANES : (t + 1) * LANES], 1.0, 0.0) for kind in kinds for t in range(tiles)
    ]
    stacked = jnp.concatenate(parts, axis=0)
    down = lax.broadcasted_iota(jnp.int32, (LANES, LANES), 0)
    along = lax.broadcasted_iota(jnp.int32, (LANES, LANES), 1)
    within = product(stacked, jnp.where(down < along, 1.0, 0.0))
    totals = product(stacked, jnp.ones((LANES, LANES), jnp.float32))
    ranks, sums = [], []
    for kind in range(3):
        base = jnp.zeros((1, LANES), jnp.float32)
        row_ranks = []
        for t in range(tiles):
            at = kind * tiles + t
            row_ranks.append(within[at : at + 1] + base)
            base = base + totals[at : at + 1]
        ranks.append(row_ranks)
        sums.append(base)
    spots = []
    for t in range(tiles):
        at = slice(t * LANES, (t + 1) * LANES)
        spots.append(
            jnp.where(
                kinds[0][:, at],
                ranks[0][t],
                jnp.where(kinds[1][:, at], width - sums[1] + ranks[1][t], sums[0] + ranks[2][t]),
            )
        )
    return jnp.concatenate(spots, axis=1), jnp.maximum(sums[0], sums[1])


def one_hot(spots, low, count):
    width = spots.shape[1]
    down = lax.broadcasted_iota(jnp.int32, (count, width), 0) + low
    return jnp.where(spots.astype(jnp.int32) == down, 1.0, 0.0).astype(jnp.bfloat16)


def each_tile(width):
    def run(body):
        for low in range(0, width, TILE):
            body(low)

    return run


def put_halo(tail, head, value, low, width):
    rows = value.shape[0]
    half = width // 2
    lane = lax.broadcasted_iota(jnp.int32, (1, LANES), 1)
    for row in range(2):
        if low < half:
            tail[:, pl.ds(row * half + low, TILE)] = value[rows - 2 + row].astype(jnp.bfloat16)
        else:
            head[:, pl.ds(row * half + low - half, TILE)] = value[row].astype(jnp.bfloat16)
    if low == half:
        first, second = (value[rows - 2 + row, :, :LANES].astype(jnp.float32) for row in range(2))
        mixed = jnp.where(lane < SPARE, first, pltpu.roll(second, SPARE, 1))
        tail[:, pl.ds(width, LANES)] = mixed.astype(jnp.bfloat16)
    if low + TILE == half:
        first, second = (value[row, :, TILE - LANES :].astype(jnp.float32) for row in range(2))
        mixed = jnp.where(lane < SPARE, pltpu.roll(first, SPARE, 1), second)
        head[:, pl.ds(width, LANES)] = mixed.astype(jnp.bfloat16)


def sort_body(meta, lattice, start, *refs):
    hot, main, most, to_next, to_last, spots_at = refs
    rows, cells, width = start.shape
    spots, larger = places(lattice[0:1, :])
    most[...] = jnp.broadcast_to(larger, most.shape)
    spots_at[...] = jnp.broadcast_to(spots, spots_at.shape)
    narrow = start[...].astype(jnp.bfloat16).reshape(rows * cells, width)

    @each_tile(width)
    def _(low):
        some = one_hot(spots_at[0:1, :], low, TILE)
        at = pl.ds(low, TILE)
        hot[at, :] = some
        value = product_t(narrow, some).astype(jnp.bfloat16).reshape(rows, cells, TILE)
        main[:, :, at] = value
        put_halo(to_next, to_last, value, low, width)


def weights_body(meta, hot, lattice, weights):
    del meta
    both = lattice[...].astype(jnp.float32).astype(jnp.bfloat16)
    sorted_both = product_t(both, hot[...])
    speed = jnp.abs(sorted_both) * lattice_speed
    weights[0:1, :] = -1.5 * (speed[0:1] + speed[1:2])
    weights[1:2, :] = 2.0 * speed[0:1]
    weights[2:3, :] = -0.5 * speed[0:1]
    weights[3:4, :] = 2.0 * speed[1:2]
    weights[4:5, :] = -0.5 * speed[1:2]
    weights[5:7, :] = sorted_both
    weights[7:8, :] = jnp.zeros_like(speed[0:1])


def rest_body(meta, collision, hot, token, out):
    del meta, token
    rows, cells, width = collision.shape
    narrow = collision[...].astype(jnp.bfloat16).reshape(rows * cells, width)

    @each_tile(width)
    def _(low):
        at = pl.ds(low, TILE)
        out[:, :, at] = product_t(narrow, hot[at, :]).astype(jnp.bfloat16).reshape(rows, cells, TILE)


def inverse_body(meta, lattice, most, inverse, hot, own_last, other_last, own, other, token, crowded, hot_other, spots_at):
    width = hot.shape[0]
    spots, larger = places(lattice[0:1, :])
    largest = jnp.maximum(most[...], larger)
    token[...] = largest
    crowded[0] = (jnp.max(largest) > float(width // 2 + SPARE)).astype(jnp.int32)
    spots_at[...] = jnp.broadcast_to(spots, spots_at.shape)

    @each_tile(width)
    def _(low):
        hot_other[pl.ds(low, TILE), :] = one_hot(spots_at[0:1, :], low, TILE)

    for source, last, final, place in (
        (hot, own_last, own, meta[0]),
        (hot_other, other_last, other, 1 - meta[0]),
    ):
        columns = pl.ds(pl.multiple_of(place * width, width), width)

        for low in range(0, width, TILE):
            at = pl.ds(low, TILE)
            value = product_t(source[at, :], inverse[:, columns]).astype(jnp.bfloat16)
            last[at, :] = value
            for far in range(0, width, TILE):
                to = pl.ds(far, TILE)
                final[at, to] = product_t(value, hot[to, :]).astype(jnp.bfloat16)


def drift_at(row, at, region, refs, left, right):
    field, before, after, weights = refs
    rows, size, _ = field.shape
    centre = field[row, :, at]

    def behind(step):
        source = row - step
        if source >= 0:
            return field[source, :, at].astype(jnp.float32)
        return left[2 + source]

    def ahead(step):
        source = row + step
        if source < rows:
            return field[source, :, at].astype(jnp.float32)
        return right[source - rows]

    def one(step):
        if region == 0:
            return behind(step)
        if region == 2:
            return ahead(step)
        return jnp.where(weights[5:6, at] > 0.0, behind(step), ahead(step))

    long = jnp.concatenate(
        [
            before[row, before.shape[1] - EDGE :, at].astype(jnp.float32),
            centre.astype(jnp.float32),
            after[row, 0:EDGE, at].astype(jnp.float32),
        ],
        axis=0,
    )
    centre = centre.astype(jnp.float32)
    up = weights[6:7, at] > 0.0

    def beside(step):
        return jnp.where(up, long[EDGE - step : EDGE - step + size], long[EDGE + step : EDGE + step + size])

    total = weights[0:1, at] * centre
    total = total + weights[1:2, at] * one(1) + weights[2:3, at] * one(2)
    total = total + weights[3:4, at] * beside(1) + weights[4:5, at] * beside(2)
    return centre, total


def halo_rows(halo, width, low, half):
    if 0 <= low < half:
        return [halo[:, pl.ds(row * half + low, LANES)].astype(jnp.float32) for row in range(2)]
    mixed = halo[:, pl.ds(width, LANES)].astype(jnp.float32)
    other = pltpu.roll(mixed, SPARE, 1)
    return [mixed, other] if low >= half else [other, mixed]


def drifts(fields, refs, body):
    weights, from_last, from_next = refs[:3]
    rows, _, width = fields[0].shape
    half = width // 2
    ends = (0, half // LANES - 1, half // LANES + 1, width // LANES)
    for region in range(3):

        for index in range(ends[region], ends[region + 1]):
            at = pl.ds(index * LANES, LANES)
            left, right = None, None
            if region < 2:
                left = halo_rows(from_last, width, index * LANES, half)
            if region > 0:
                right = halo_rows(from_next, width, index * LANES - half, half)
            for row in range(rows):
                body((row, slice(None), at), *drift_at(row, at, region, (*fields, weights), left, right))


def part(ref, index):
    size = ref.shape[1] // CHUNKS
    return ref.at[:, pl.ds(index % CHUNKS * size, size), :]


def stage_one(index):
    def kernel(meta, start, *refs):
        del meta
        weights, from_last, from_next, _, rounded, drift = refs
        size = from_last.shape[0] // CHUNKS
        ys = pl.ds(index * size, size)
        around = weights, from_last.at[ys, :], from_next.at[ys, :]

        def body(at, centre, total):
            drift[at] = total
            rounded[at] = (centre + step_half * total).astype(jnp.bfloat16)

        drifts((part(start, index), part(start, index - 1), part(start, index + 1)), around, body)

    return kernel


def stage_two(index):
    def kernel(meta, field, before, after, *refs):
        del meta
        start, collision, drift, rounded_one, rounded, part_one, part_two = refs[3:]
        start, collision = part(start, index), part(collision, index)

        def body(at, centre, total):
            rounded[at] = (centre + step_half * total).astype(jnp.bfloat16)
            change = centre - rounded_one[at].astype(jnp.float32)
            zero = drift[at] + collision[at].astype(jnp.float32)
            base = start[at].astype(jnp.float32)
            part_one[at] = base + (5.0 / 48.0) * zero + (1.0 / 6.0) * total - (1.0 / 3.0) * change
            part_two[at] = (2.0 / 3.0) * change - (1.0 / 48.0) * zero - (1.0 / 12.0) * total

        drifts((field, before, after), refs, body)

    return kernel


def stage_three(index):
    del index

    def kernel(meta, field, before, after, *refs):
        del meta
        rounded_two, part_one, part_two, rounded, rest = refs[3:]

        def body(at, centre, total):
            change = centre - rounded_two[at].astype(jnp.float32)
            rounded[at] = (part_one[at] - (1.0 / 48.0) * total - (1.0 / 12.0) * change).astype(jnp.bfloat16)
            rest[at] = part_two[at] + (5.0 / 48.0) * total - (7.0 / 12.0) * change

        drifts((field, before, after), refs, body)

    return kernel


def stage_four(index):
    del index

    def kernel(meta, field, before, after, *refs):
        del meta
        rest, rounded = refs[3:]

        def body(at, centre, total):
            rounded[at] = (centre + step_half * total + rest[at]).astype(jnp.bfloat16)

        drifts((field, before, after), refs, body)

    return kernel


def collide_body(meta, mine, beside, own, other, field, to_next, to_last, token):
    del meta
    rows, size, width = field.shape

    @each_tile(width)
    def _(low):
        at = pl.ds(low, TILE)
        first = mine[...].reshape(rows * size, width)
        second = beside[...].reshape(rows * size, width)
        result = (product(first, own[:, at]) + product(second, other[:, at])).reshape(rows, size, TILE)
        field[:, :, at] = result
        put_halo(to_next, to_last, result, low, width)

    token[...] = jnp.zeros_like(token)


def unsort_body(meta, rounded, hot, plain):
    del meta
    rows, size, width = rounded.shape
    first = rounded[...].reshape(rows * size, width)

    @each_tile(width)
    def _(low):
        at = pl.ds(low, TILE)
        plain[:, :, at] = product(first, hot[:, at]).astype(jnp.bfloat16).reshape(rows, size, TILE)


def last_body(*refs):
    mine, beside, plain = refs[:CHUNKS], refs[CHUNKS : 2 * CHUNKS], refs[2 * CHUNKS : 3 * CHUNKS]
    own, other, field, collision = refs[3 * CHUNKS :]
    at = pl.ds(pl.multiple_of(pl.program_id(0) * TILE, TILE), TILE)
    for index in range(CHUNKS):
        rows, size, width = mine[index].shape
        first = mine[index][...].reshape(rows * size, width)
        second = beside[index][...].reshape(rows * size, width)
        result = (product(first, own[:, at]) + product(second, other[:, at])).reshape(rows, size, TILE)
        ys = pl.ds(index * size, size)
        field[:, ys, :] = result
        collision[:, ys, :] = (result - plain[index][:, :, at].astype(jnp.float32)) * (1.0 / step_half)


def sorted_path(start_field, start_collision, inverse, lattice):
    rows, cells, width = start_field.shape
    size = cells // CHUNKS
    count = lax.axis_size("gx")
    forth = [(i, (i + 1) % count) for i in range(count)]
    back = [((i + 1) % count, i) for i in range(count)]
    meta = lax.axis_index("vert").astype(jnp.int32).reshape(1)
    narrow = jnp.bfloat16

    def shape(dims, dtype=jnp.float32):
        return jax.ShapeDtypeStruct(dims, dtype)

    halo_shape = shape((size, width + LANES), narrow)
    square = shape((width, width), narrow)
    wide_shape = shape((rows, size, width))
    thin_shape = shape((rows, size, width), narrow)
    token_shape = shape((8, LANES))
    elements = rows * size * width

    def exchange(to_next, to_last, turn=0):
        if turn % 2:
            from_next = lax.ppermute(to_last, "gx", back)
            return lax.ppermute(to_next, "gx", forth), from_next
        from_last = lax.ppermute(to_next, "gx", forth)
        return from_last, lax.ppermute(to_last, "gx", back)

    beside_lattice = swap(lattice)
    hot, main, most, *ends = call(
        sort_body,
        [square, shape((rows, cells, width), narrow), token_shape] + [shape((cells, width + LANES), narrow)] * 2,
        (4 * elements * width, 16 * elements),
        meta,
        (lattice, start_field),
        [pltpu.VMEM((8, width), jnp.float32)],
    )
    halos = [exchange(*ends)] * CHUNKS
    (weights,) = call(weights_body, [shape((8, width))], (1, 1), meta, (hot, lattice))
    own_last, other_last, own, other, largest, crowded = call(
        inverse_body,
        [square] * 4 + [token_shape, shape((1,), jnp.int32)],
        (8 * width**3, 20 * width**2),
        meta,
        (beside_lattice, most, inverse, hot),
        [pltpu.VMEM((width, width), narrow), pltpu.VMEM((8, width), jnp.float32)],
    )

    def stage(body, outs, fields, index, *extra):
        kernel = body(index)
        place = 1 + len(fields)
        if index % 2:

            def ordered(meta, *refs):
                refs = list(refs)
                refs[place], refs[place + 1] = refs[place + 1], refs[place]
                kernel(meta, *refs)

        else:
            ordered = kernel
        return call(
            ordered,
            outs,
            (30 * elements, 16 * elements),
            meta,
            (*fields, weights, *halos[index][:: -1 if index % 2 else 1], *extra),
        )

    def advance(rounded):
        results = [
            call(
                collide_body,
                [wide_shape, halo_shape, halo_shape, token_shape],
                (4 * elements * width, 8 * elements + 4 * width * width),
                meta,
                (r, swap(r), own, other),
            )
            for r in rounded
        ]
        return [r[0] for r in results], [exchange(r[1], r[2], turn) for turn, r in enumerate(results)], results[-1][3]

    def around(index):
        return fields[index], fields[index - 1], fields[(index + 1) % CHUNKS]

    every = range(CHUNKS)
    kept = [stage(stage_one, [thin_shape, wide_shape], (main,), i, largest) for i in every]
    fields, halos, token = advance([k[0] for k in kept])
    (collision,) = call(
        rest_body,
        [shape((rows, cells, width), narrow)],
        (2 * CHUNKS * elements * width, 6 * CHUNKS * elements),
        meta,
        (start_collision, hot, token),
    )
    kept = [
        stage(
            stage_two, [thin_shape, wide_shape, wide_shape], around(i), i, main, collision, kept[i][1], kept[i][0]
        )
        for i in every
    ]
    fields, halos, token = advance([k[0] for k in kept])
    kept = [stage(stage_three, [thin_shape, wide_shape], around(i), i, *kept[i]) for i in every]
    fields, halos, token = advance([k[0] for k in kept])
    rounded = [stage(stage_four, [thin_shape], around(i), i, kept[i][1])[0] for i in every]
    beside = [swap(r) for r in rounded]
    plain = [
        call(unsort_body, [thin_shape], (2 * elements * width, 4 * elements), meta, (r, hot))[0] for r in rounded
    ]
    operands = (*rounded, *beside, *plain, own_last, other_last)
    ends = pl.pallas_call(
        last_body,
        grid=(width // TILE,),
        out_shape=[shape((rows, cells, width))] * 2,
        in_specs=[pl.BlockSpec(memory_space=pltpu.VMEM)] * len(operands),
        out_specs=[pl.BlockSpec((rows, cells, TILE), lambda i: (0, 0, i))] * 2,
        compiler_params=pltpu.CompilerParams(vmem_limit_bytes=16 * MIB),
        cost_estimate=pl.CostEstimate(
            flops=4 * CHUNKS * elements * width, bytes_accessed=12 * CHUNKS * elements, transcendentals=0
        ),
    )(*operands)
    return (*ends, crowded)


def per_device(start_field, start_collision, inverse, lattice):
    width = start_field.shape[2]
    field, collision, crowded = sorted_path(start_field, start_collision, inverse, lattice)

    def again(state):
        here = lax.axis_index("vert")
        mine = lax.dynamic_slice_in_dim(inverse, here * width, width, axis=1)
        other = lax.dynamic_slice_in_dim(inverse, (1 - here) * width, width, axis=1)
        return (*general(start_field, start_collision, mine, other, lattice), jnp.zeros((1,), jnp.int32))

    field, collision, _ = lax.while_loop(lambda state: state[2][0] > 0, again, (field, collision, crowded))
    return field, collision


def solution(mesh):
    return jax.shard_map(
        per_device,
        mesh=mesh,
        in_specs=(P("gx", None, "vert"), P("gx", None, "vert"), P("vert", None), P(None, "vert")),
        out_specs=(P("gx", None, "vert"), P("gx", None, "vert")),
        check_vma=False,
    )
```

```python
import jax
import jax.numpy as jnp
from jax import lax
from jax.experimental import pallas as pl
from jax.experimental.pallas import tpu as pltpu
from jax.sharding import PartitionSpec as P

CHUNKS = 2

step_half = 0.25
lattice_speed = 0.07

LANES = 128
EDGE = 8
MIB = 1 << 20


def padded_2(cells, axis):
    count = lax.axis_size(axis)
    head = cells[:2].astype(jnp.bfloat16)
    tail = cells[-2:].astype(jnp.bfloat16)
    return jnp.concatenate(
        [
            lax.ppermute(tail, axis, [(i, (i + 1) % count) for i in range(count)]).astype(cells.dtype),
            cells,
            lax.ppermute(head, axis, [((i + 1) % count, i) for i in range(count)]).astype(cells.dtype),
        ],
        axis=0,
    )


def upwind(minus_two, minus_one, centre, plus_one, plus_two, lattice_row):
    speed = lattice_row.astype(jnp.float32) * lattice_speed
    backward = 1.5 * centre - 2.0 * minus_one + 0.5 * minus_two
    forward = -1.5 * centre + 2.0 * plus_one - 0.5 * plus_two
    return jnp.where(lattice_row > 0, speed * backward, speed * forward)


def transport(field, lattice):
    padded = padded_2(field, "gx")
    rows = field.shape[0]
    flux_x = upwind(
        padded[0:rows],
        padded[1 : rows + 1],
        field,
        padded[3 : rows + 3],
        padded[4 : rows + 4],
        lattice[0],
    )
    flux_y = upwind(
        jnp.roll(field, 2, 1),
        jnp.roll(field, 1, 1),
        field,
        jnp.roll(field, -1, 1),
        jnp.roll(field, -2, 1),
        lattice[1],
    )
    return -(flux_x + flux_y)


def swap(cells):
    return lax.ppermute(cells, "vert", [(0, 1), (1, 0)])


SUBSTEPS = (
    (5.0 / 48.0, 0.0, -1.0 / 48.0, 0.0, 1.0, step_half, 0.0, 0.0),
    (1.0 / 6.0, -1.0 / 3.0, -1.0 / 12.0, 2.0 / 3.0, 1.0, step_half, 0.0, 0.0),
    (-1.0 / 48.0, -1.0 / 12.0, 5.0 / 48.0, -7.0 / 12.0, 0.0, 0.0, 1.0, 0.0),
    (0.0, 0.0, 0.0, 0.0, 1.0, step_half, 0.0, 1.0),
)


def general(start_field, start_collision, mine, other, lattice):
    table = jnp.array(SUBSTEPS, jnp.float32)

    def substep(index, state):
        field, rounded, third, fourth = state
        weight = lax.dynamic_index_in_dim(table, index, 0, keepdims=False)
        drift = transport(field, lattice)
        change = field - rounded
        third = third + weight[0] * drift + weight[1] * change
        fourth = fourth + weight[2] * drift + weight[3] * change
        value = weight[4] * field + weight[5] * drift + weight[6] * third + weight[7] * fourth
        rounded = lax.reduce_precision(value, 8, 7)
        narrow = rounded.astype(jnp.bfloat16)
        field = jnp.einsum("xyw,vw->xyv", narrow, mine, preferred_element_type=jnp.float32) + jnp.einsum(
            "xyw,vw->xyv", swap(narrow), other, preferred_element_type=jnp.float32
        )
        return field, rounded, third, fourth

    third = start_field + (5.0 / 48.0) * start_collision
    fourth = (-1.0 / 48.0) * start_collision
    field, rounded, _, _ = lax.fori_loop(0, len(SUBSTEPS), substep, (start_field, start_field, third, fourth))
    return field, (field - rounded) * (1.0 / step_half)


SPARE = LANES // 2


def call(body, outs, cost, meta, operands, scratch=()):
    return pl.pallas_call(
        body,
        out_shape=outs,
        in_specs=[pl.BlockSpec(memory_space=pltpu.SMEM)] + [pl.BlockSpec(memory_space=pltpu.VMEM)] * len(operands),
        out_specs=[
            pl.BlockSpec(memory_space=pltpu.SMEM if out.shape == (1,) else pltpu.VMEM) for out in outs
        ],
        scratch_shapes=list(scratch),
        compiler_params=pltpu.CompilerParams(vmem_limit_bytes=16 * MIB),
        cost_estimate=pl.CostEstimate(flops=cost[0], bytes_accessed=cost[1], transcendentals=0),
    )(meta, *operands)


TILE = 256


def product(left, right):
    return lax.dot_general(left, right, (((1,), (0,)), ((), ())), preferred_element_type=jnp.float32)


def product_t(left, right):
    return lax.dot_general(left, right, (((1,), (1,)), ((), ())), preferred_element_type=jnp.float32)


def places(row):
    width = row.shape[1]
    tiles = width // LANES
    value = row.astype(jnp.float32)
    kinds = [value > 0.0, value < 0.0, value == 0.0]
    parts = [
        jnp.where(kind[:, t * LANES : (t + 1) * LANES], 1.0, 0.0) for kind in kinds for t in range(tiles)
    ]
    stacked = jnp.concatenate(parts, axis=0)
    down = lax.broadcasted_iota(jnp.int32, (LANES, LANES), 0)
    along = lax.broadcasted_iota(jnp.int32, (LANES, LANES), 1)
    within = product(stacked, jnp.where(down < along, 1.0, 0.0))
    totals = product(stacked, jnp.ones((LANES, LANES), jnp.float32))
    ranks, sums = [], []
    for kind in range(3):
        base = jnp.zeros((1, LANES), jnp.float32)
        row_ranks = []
        for t in range(tiles):
            at = kind * tiles + t
            row_ranks.append(within[at : at + 1] + base)
            base = base + totals[at : at + 1]
        ranks.append(row_ranks)
        sums.append(base)
    spots = []
    for t in range(tiles):
        at = slice(t * LANES, (t + 1) * LANES)
        spots.append(
            jnp.where(
                kinds[0][:, at],
                ranks[0][t],
                jnp.where(kinds[1][:, at], width - sums[1] + ranks[1][t], sums[0] + ranks[2][t]),
            )
        )
    return jnp.concatenate(spots, axis=1), jnp.maximum(sums[0], sums[1])


def one_hot(spots, low, count):
    width = spots.shape[1]
    down = lax.broadcasted_iota(jnp.int32, (count, width), 0) + low
    return jnp.where(spots.astype(jnp.int32) == down, 1.0, 0.0).astype(jnp.bfloat16)


def each_tile(width):
    def run(body):
        for low in range(0, width, TILE):
            body(low)

    return run


def put_halo(tail, head, value, low, width):
    rows = value.shape[0]
    half = width // 2
    lane = lax.broadcasted_iota(jnp.int32, (1, LANES), 1)
    for row in range(2):
        if low < half:
            tail[:, pl.ds(row * half + low, TILE)] = value[rows - 2 + row].astype(jnp.bfloat16)
        else:
            head[:, pl.ds(row * half + low - half, TILE)] = value[row].astype(jnp.bfloat16)
    if low == half:
        first, second = (value[rows - 2 + row, :, :LANES].astype(jnp.float32) for row in range(2))
        mixed = jnp.where(lane < SPARE, first, pltpu.roll(second, SPARE, 1))
        tail[:, pl.ds(width, LANES)] = mixed.astype(jnp.bfloat16)
    if low + TILE == half:
        first, second = (value[row, :, TILE - LANES :].astype(jnp.float32) for row in range(2))
        mixed = jnp.where(lane < SPARE, pltpu.roll(first, SPARE, 1), second)
        head[:, pl.ds(width, LANES)] = mixed.astype(jnp.bfloat16)


def sort_body(meta, lattice, start, *refs):
    hot, main, most, to_next, to_last, spots_at = refs
    rows, cells, width = start.shape
    spots, larger = places(lattice[0:1, :])
    most[...] = jnp.broadcast_to(larger, most.shape)
    spots_at[...] = jnp.broadcast_to(spots, spots_at.shape)
    narrow = start[...].astype(jnp.bfloat16).reshape(rows * cells, width)

    @each_tile(width)
    def _(low):
        some = one_hot(spots_at[0:1, :], low, TILE)
        at = pl.ds(low, TILE)
        hot[at, :] = some
        value = product_t(narrow, some).astype(jnp.bfloat16).reshape(rows, cells, TILE)
        main[:, :, at] = value
        put_halo(to_next, to_last, value, low, width)


def weights_body(meta, hot, lattice, weights):
    del meta
    both = lattice[...].astype(jnp.float32).astype(jnp.bfloat16)
    sorted_both = product_t(both, hot[...])
    speed = jnp.abs(sorted_both) * lattice_speed
    weights[0:1, :] = -1.5 * (speed[0:1] + speed[1:2])
    weights[1:2, :] = 2.0 * speed[0:1]
    weights[2:3, :] = -0.5 * speed[0:1]
    weights[3:4, :] = 2.0 * speed[1:2]
    weights[4:5, :] = -0.5 * speed[1:2]
    weights[5:7, :] = sorted_both
    weights[7:8, :] = jnp.zeros_like(speed[0:1])


def rest_body(meta, collision, hot, token, out):
    del meta, token
    rows, cells, width = collision.shape
    narrow = collision[...].astype(jnp.bfloat16).reshape(rows * cells, width)

    @each_tile(width)
    def _(low):
        at = pl.ds(low, TILE)
        out[:, :, at] = product_t(narrow, hot[at, :]).astype(jnp.bfloat16).reshape(rows, cells, TILE)


def inverse_body(meta, lattice, most, inverse, hot, own_last, other_last, own, other, token, crowded, hot_other, spots_at):
    width = hot.shape[0]
    spots, larger = places(lattice[0:1, :])
    largest = jnp.maximum(most[...], larger)
    token[...] = largest
    crowded[0] = (jnp.max(largest) > float(width // 2 + SPARE)).astype(jnp.int32)
    spots_at[...] = jnp.broadcast_to(spots, spots_at.shape)

    @each_tile(width)
    def _(low):
        hot_other[pl.ds(low, TILE), :] = one_hot(spots_at[0:1, :], low, TILE)

    for source, last, final, place in (
        (hot, own_last, own, meta[0]),
        (hot_other, other_last, other, 1 - meta[0]),
    ):
        columns = pl.ds(pl.multiple_of(place * width, width), width)

        for low in range(0, width, TILE):
            at = pl.ds(low, TILE)
            value = product_t(source[at, :], inverse[:, columns]).astype(jnp.bfloat16)
            last[at, :] = value
            for far in range(0, width, TILE):
                to = pl.ds(far, TILE)
                final[at, to] = product_t(value, hot[to, :]).astype(jnp.bfloat16)


def drift_at(row, at, region, refs, left, right):
    field, before, after, weights = refs
    rows, size, _ = field.shape
    centre = field[row, :, at]

    def behind(step):
        source = row - step
        if source >= 0:
            return field[source, :, at].astype(jnp.float32)
        return left[2 + source]

    def ahead(step):
        source = row + step
        if source < rows:
            return field[source, :, at].astype(jnp.float32)
        return right[source - rows]

    def one(step):
        if region == 0:
            return behind(step)
        if region == 2:
            return ahead(step)
        return jnp.where(weights[5:6, at] > 0.0, behind(step), ahead(step))

    long = jnp.concatenate(
        [
            before[row, before.shape[1] - EDGE :, at].astype(jnp.float32),
            centre.astype(jnp.float32),
            after[row, 0:EDGE, at].astype(jnp.float32),
        ],
        axis=0,
    )
    centre = centre.astype(jnp.float32)
    up = weights[6:7, at] > 0.0

    def beside(step):
        return jnp.where(up, long[EDGE - step : EDGE - step + size], long[EDGE + step : EDGE + step + size])

    total = weights[0:1, at] * centre
    total = total + weights[1:2, at] * one(1) + weights[2:3, at] * one(2)
    total = total + weights[3:4, at] * beside(1) + weights[4:5, at] * beside(2)
    return centre, total


def halo_rows(halo, width, low, half):
    if 0 <= low < half:
        return [halo[:, pl.ds(row * half + low, LANES)].astype(jnp.float32) for row in range(2)]
    mixed = halo[:, pl.ds(width, LANES)].astype(jnp.float32)
    other = pltpu.roll(mixed, SPARE, 1)
    return [mixed, other] if low >= half else [other, mixed]


def drifts(fields, refs, body):
    weights, from_last, from_next = refs[:3]
    rows, _, width = fields[0].shape
    half = width // 2
    ends = (0, half // LANES - 1, half // LANES + 1, width // LANES)
    for region in range(3):

        for index in range(ends[region], ends[region + 1]):
            at = pl.ds(index * LANES, LANES)
            left, right = None, None
            if region < 2:
                left = halo_rows(from_last, width, index * LANES, half)
            if region > 0:
                right = halo_rows(from_next, width, index * LANES - half, half)
            for row in range(rows):
                body((row, slice(None), at), *drift_at(row, at, region, (*fields, weights), left, right))


def part(ref, index):
    size = ref.shape[1] // CHUNKS
    return ref.at[:, pl.ds(index % CHUNKS * size, size), :]


def stage_one(index):
    def kernel(meta, start, *refs):
        del meta
        weights, from_last, from_next, _, rounded, drift = refs
        size = from_last.shape[0] // CHUNKS
        ys = pl.ds(index * size, size)
        around = weights, from_last.at[ys, :], from_next.at[ys, :]

        def body(at, centre, total):
            drift[at] = total
            rounded[at] = (centre + step_half * total).astype(jnp.bfloat16)

        drifts((part(start, index), part(start, index - 1), part(start, index + 1)), around, body)

    return kernel


def stage_two(index):
    def kernel(meta, field, before, after, *refs):
        del meta
        start, collision, drift, rounded_one, rounded, part_one, part_two = refs[3:]
        start, collision = part(start, index), part(collision, index)

        def body(at, centre, total):
            rounded[at] = (centre + step_half * total).astype(jnp.bfloat16)
            change = centre - rounded_one[at].astype(jnp.float32)
            zero = drift[at] + collision[at].astype(jnp.float32)
            base = start[at].astype(jnp.float32)
            part_one[at] = base + (5.0 / 48.0) * zero + (1.0 / 6.0) * total - (1.0 / 3.0) * change
            part_two[at] = (2.0 / 3.0) * change - (1.0 / 48.0) * zero - (1.0 / 12.0) * total

        drifts((field, before, after), refs, body)

    return kernel


def stage_three(index):
    del index

    def kernel(meta, field, before, after, *refs):
        del meta
        rounded_two, part_one, part_two, rounded, rest = refs[3:]

        def body(at, centre, total):
            change = centre - rounded_two[at].astype(jnp.float32)
            rounded[at] = (part_one[at] - (1.0 / 48.0) * total - (1.0 / 12.0) * change).astype(jnp.bfloat16)
            rest[at] = part_two[at] + (5.0 / 48.0) * total - (7.0 / 12.0) * change

        drifts((field, before, after), refs, body)

    return kernel


def stage_four(index):
    del index

    def kernel(meta, field, before, after, *refs):
        del meta
        rest, rounded = refs[3:]

        def body(at, centre, total):
            rounded[at] = (centre + step_half * total + rest[at]).astype(jnp.bfloat16)

        drifts((field, before, after), refs, body)

    return kernel


def collide_body(meta, mine, beside, own, other, field, to_next, to_last, token):
    del meta
    rows, size, width = field.shape

    @each_tile(width)
    def _(low):
        at = pl.ds(low, TILE)
        first = mine[...].reshape(rows * size, width)
        second = beside[...].reshape(rows * size, width)
        result = (product(first, own[:, at]) + product(second, other[:, at])).reshape(rows, size, TILE)
        field[:, :, at] = result
        put_halo(to_next, to_last, result, low, width)

    token[...] = jnp.zeros_like(token)


def unsort_body(meta, rounded, hot, plain):
    del meta
    rows, size, width = rounded.shape
    first = rounded[...].reshape(rows * size, width)

    @each_tile(width)
    def _(low):
        at = pl.ds(low, TILE)
        plain[:, :, at] = product(first, hot[:, at]).astype(jnp.bfloat16).reshape(rows, size, TILE)


def last_body(*refs):
    mine, beside, plain = refs[:CHUNKS], refs[CHUNKS : 2 * CHUNKS], refs[2 * CHUNKS : 3 * CHUNKS]
    own, other, field, collision = refs[3 * CHUNKS :]
    at = pl.ds(pl.multiple_of(pl.program_id(0) * TILE, TILE), TILE)
    for index in range(CHUNKS):
        rows, size, width = mine[index].shape
        first = mine[index][...].reshape(rows * size, width)
        second = beside[index][...].reshape(rows * size, width)
        result = (product(first, own[:, at]) + product(second, other[:, at])).reshape(rows, size, TILE)
        ys = pl.ds(index * size, size)
        field[:, ys, :] = result
        collision[:, ys, :] = (result - plain[index][:, :, at].astype(jnp.float32)) * (1.0 / step_half)


def sorted_path(start_field, start_collision, inverse, lattice):
    rows, cells, width = start_field.shape
    size = cells // CHUNKS
    count = lax.axis_size("gx")
    forth = [(i, (i + 1) % count) for i in range(count)]
    back = [((i + 1) % count, i) for i in range(count)]
    meta = lax.axis_index("vert").astype(jnp.int32).reshape(1)
    narrow = jnp.bfloat16

    def shape(dims, dtype=jnp.float32):
        return jax.ShapeDtypeStruct(dims, dtype)

    halo_shape = shape((size, width + LANES), narrow)
    square = shape((width, width), narrow)
    wide_shape = shape((rows, size, width))
    thin_shape = shape((rows, size, width), narrow)
    token_shape = shape((8, LANES))
    elements = rows * size * width

    def exchange(to_next, to_last, turn=0):
        if turn % 2:
            from_next = lax.ppermute(to_last, "gx", back)
            return lax.ppermute(to_next, "gx", forth), from_next
        from_last = lax.ppermute(to_next, "gx", forth)
        return from_last, lax.ppermute(to_last, "gx", back)

    beside_lattice = swap(lattice)
    hot, main, most, *ends = call(
        sort_body,
        [square, shape((rows, cells, width), narrow), token_shape] + [shape((cells, width + LANES), narrow)] * 2,
        (4 * elements * width, 16 * elements),
        meta,
        (lattice, start_field),
        [pltpu.VMEM((8, width), jnp.float32)],
    )
    halos = [exchange(*ends)] * CHUNKS
    (weights,) = call(weights_body, [shape((8, width))], (1, 1), meta, (hot, lattice))
    own_last, other_last, own, other, largest, crowded = call(
        inverse_body,
        [square] * 4 + [token_shape, shape((1,), jnp.int32)],
        (8 * width**3, 20 * width**2),
        meta,
        (beside_lattice, most, inverse, hot),
        [pltpu.VMEM((width, width), narrow), pltpu.VMEM((8, width), jnp.float32)],
    )

    def stage(body, outs, fields, index, *extra):
        kernel = body(index)
        place = 1 + len(fields)
        if index % 2:

            def ordered(meta, *refs):
                refs = list(refs)
                refs[place], refs[place + 1] = refs[place + 1], refs[place]
                kernel(meta, *refs)

        else:
            ordered = kernel
        return call(
            ordered,
            outs,
            (30 * elements, 16 * elements),
            meta,
            (*fields, weights, *halos[index][:: -1 if index % 2 else 1], *extra),
        )

    def advance(rounded):
        results = [
            call(
                collide_body,
                [wide_shape, halo_shape, halo_shape, token_shape],
                (4 * elements * width, 8 * elements + 4 * width * width),
                meta,
                (r, swap(r), own, other),
            )
            for r in rounded
        ]
        return [r[0] for r in results], [exchange(r[1], r[2], turn) for turn, r in enumerate(results)], results[-1][3]

    def around(index):
        return fields[index], fields[index - 1], fields[(index + 1) % CHUNKS]

    every = range(CHUNKS)
    (collision,) = call(
        rest_body,
        [shape((rows, cells, width), narrow)],
        (2 * CHUNKS * elements * width, 6 * CHUNKS * elements),
        meta,
        (start_collision, hot, largest),
    )
    kept = [stage(stage_one, [thin_shape, wide_shape], (main,), i, collision) for i in every]
    fields, halos, token = advance([k[0] for k in kept])
    kept = [
        stage(
            stage_two, [thin_shape, wide_shape, wide_shape], around(i), i, main, collision, kept[i][1], kept[i][0]
        )
        for i in every
    ]
    fields, halos, token = advance([k[0] for k in kept])
    kept = [stage(stage_three, [thin_shape, wide_shape], around(i), i, *kept[i]) for i in every]
    fields, halos, token = advance([k[0] for k in kept])
    rounded = [stage(stage_four, [thin_shape], around(i), i, kept[i][1])[0] for i in every]
    beside = [swap(r) for r in rounded]
    plain = [
        call(unsort_body, [thin_shape], (2 * elements * width, 4 * elements), meta, (r, hot))[0] for r in rounded
    ]
    operands = (*rounded, *beside, *plain, own_last, other_last)
    ends = pl.pallas_call(
        last_body,
        grid=(width // TILE,),
        out_shape=[shape((rows, cells, width))] * 2,
        in_specs=[pl.BlockSpec(memory_space=pltpu.VMEM)] * len(operands),
        out_specs=[pl.BlockSpec((rows, cells, TILE), lambda i: (0, 0, i))] * 2,
        compiler_params=pltpu.CompilerParams(vmem_limit_bytes=16 * MIB),
        cost_estimate=pl.CostEstimate(
            flops=4 * CHUNKS * elements * width, bytes_accessed=12 * CHUNKS * elements, transcendentals=0
        ),
    )(*operands)
    return (*ends, crowded)


def per_device(start_field, start_collision, inverse, lattice):
    width = start_field.shape[2]
    field, collision, crowded = sorted_path(start_field, start_collision, inverse, lattice)

    def again(state):
        here = lax.axis_index("vert")
        mine = lax.dynamic_slice_in_dim(inverse, here * width, width, axis=1)
        other = lax.dynamic_slice_in_dim(inverse, (1 - here) * width, width, axis=1)
        return (*general(start_field, start_collision, mine, other, lattice), jnp.zeros((1,), jnp.int32))

    field, collision, _ = lax.while_loop(lambda state: state[2][0] > 0, again, (field, collision, crowded))
    return field, collision


def solution(mesh):
    return jax.shard_map(
        per_device,
        mesh=mesh,
        in_specs=(P("gx", None, "vert"), P("gx", None, "vert"), P("vert", None), P(None, "vert")),
        out_specs=(P("gx", None, "vert"), P("gx", None, "vert")),
        check_vma=False,
    )
```
